128 devices in a mesh: dp: 4 (over y), seq: 32 (over z, x, core).
Axes of the slice: x: 4, y: 4, z: 4, core: 2. Of those that a mesh axis runs over, the one named last changes fastest.
Arguments:
- queries: bfloat16 [4096, 8, 16, 128], P('seq', 'dp'), may hold values from -48 to 48
- keys_in: bfloat16 [4096, 8, 16, 128], P('seq', 'dp'), may hold values from -48 to 48
- values_in: bfloat16 [4096, 8, 16, 128], P('seq', 'dp'), may hold values from -6 to 6
- pair_keys: int32 [64, 27], replicated, may hold values from -1 to 63, as said below
- out_weight: bfloat16 [2048, 1536], P('seq', 'dp'), may hold values from -0.125 to 0.125
- cotangent: bfloat16 [4096, 8, 1536], P('seq', 'dp'), may hold values from -6 to 6
Outputs:
- output: bfloat16 [4096, 8, 1536], P('seq', 'dp')
- grad_queries: bfloat16 [4096, 8, 16, 128], P('seq', 'dp')
- grad_keys: bfloat16 [4096, 8, 16, 128], P('seq', 'dp')
- grad_values: bfloat16 [4096, 8, 16, 128], P('seq', 'dp')
- weight_grad: float32 [2048, 1536], P('seq', 'dp')
The draws below stay inside these ranges and needn't reach their ends.
Inputs may be any that keep to these rules, and one draw needn't show every extreme that they name: `pair_keys`: A tile's row lists the tiles whose frame, row and column tile positions each differ from its own by at most one, itself included, in increasing order, then -1 in the remaining slots; the positions of the tiles in the 4 by 4 by 4 grid are a permutation drawn anew.
All inputs are finite; a program needn't handle non-finite values.
Results may differ from the reference program's by a relative error of at most 0.022.
Values may be sent and summed in bfloat16 or wider, within the bound.
No kernel may reach another device: no remote copies, remote signals or barrier semaphores. Data moves between devices by JAX's collectives and lax.ppermute only.
A program may use at most 320 MiB of HBM per device.

```python
import jax
import jax.numpy as jnp
from jax import lax

D = 1536
HEADS = 16
HEAD_DIM = 128
TILE = 64
TILE_H = 4
TILE_W = 4
KMAX = 27
TOKENS = 4096
VIDEOS = 8
TILES = 64


def query_key_pair(key):
    draw_key = jax.random.fold_in(key, 17)
    key_one, key_two = jax.random.split(draw_key)
    full_shape = (TOKENS, VIDEOS, HEADS, HEAD_DIM)
    query_raw = jnp.clip(jax.random.normal(key_one, full_shape, jnp.float32), -6.0, 6.0)
    key_raw = jnp.clip(jax.random.normal(key_two, full_shape, jnp.float32), -6.0, 6.0)
    query_final = query_raw
    key_final = key_raw
    return (query_final, key_final)


def draw_queries(key, part):
    return query_key_pair(key)[0].astype(jnp.bfloat16)


def draw_keys_in(key, part):
    return query_key_pair(key)[1].astype(jnp.bfloat16)


def draw_pair_keys(key, part):
    position = jax.random.permutation(jax.random.fold_in(key, 29), TILES)
    plane = TILE_H * TILE_W
    frame_of = position // plane
    row_of = position // TILE_W % TILE_H
    col_of = position % TILE_W
    inside = (jnp.abs(frame_of[:, None] - frame_of[None, :]) <= 1) & (jnp.abs(row_of[:, None] - row_of[None, :]) <= 1) & (jnp.abs(col_of[:, None] - col_of[None, :]) <= 1)
    priority = jnp.where(inside, TILES - jnp.arange(TILES, dtype=jnp.int32)[None, :], 0).astype(jnp.int32)
    best_vals, best_index = lax.top_k(priority, KMAX)
    return jnp.where(best_vals > 0, best_index, -1).astype(jnp.int32)


def block_scale(own_key, dims, pieces, smallest, top_value):
    loudness, own = 1.0, jax.random.fold_in(own_key, 6)
    for dim, blocks in pieces:
        steps = jnp.exp(jax.random.uniform(jax.random.fold_in(own, dim), (blocks,), jnp.float32, smallest / len(pieces), top_value / len(pieces)))
        loudness = loudness * jnp.repeat(steps, dims[dim] // blocks).reshape([-1 if axis == dim else 1 for axis in range(len(dims))])
    return loudness


def scatter_about(own_key, extent, deviation, reach, shards=(), kind=jnp.bfloat16):
    drawn = jax.random.normal(own_key, extent, jnp.float32) * deviation
    if len(shards) > 0:
        drawn = block_scale(own_key, extent, shards, -0.22, 0.18) * drawn
    return jnp.clip(drawn, min=-reach, max=reach).astype(kind)


def setup_inputs(seed: int = 0) -> dict:
    key_of = jax.random.split(jax.random.key(seed), 7)
    queries = draw_queries(jax.random.fold_in(key_of[6], 71), 0)
    keys_in = draw_keys_in(jax.random.fold_in(key_of[6], 71), 0)
    values_in = scatter_about(key_of[2], (TOKENS, VIDEOS, HEADS, HEAD_DIM), 1.0, 6.0, ((0, 32), (1, 4)))
    pair_keys = draw_pair_keys(jax.random.fold_in(key_of[6], 71), 0)
    out_weight = scatter_about(key_of[4], (HEADS * HEAD_DIM, D), (HEADS * HEAD_DIM) ** -0.5, 0.125, ((0, 32), (1, 4)))
    cotangent = scatter_about(key_of[5], (TOKENS, VIDEOS, D), 1.0, 6.0, ((0, 32), (1, 4)))
    return {"queries": queries, "keys_in": keys_in, "values_in": values_in, "pair_keys": pair_keys, "out_weight": out_weight, "cotangent": cotangent}


def rounded(values):
    return lax.optimization_barrier(values.astype(jnp.bfloat16)).astype(jnp.float32)


def block_scores(query_block, key_block, key_index):
    score_scale = HEAD_DIM ** -0.5
    usable = key_index >= 0
    scores = jnp.einsum("qad,qkbd->qakb", query_block, key_block) * score_scale
    return jnp.where(usable[:, None, :, None], scores, -jnp.inf)


def unit_forward(query_unit, key_unit, value_unit, pair_keys):
    key_tiles = key_unit.astype(jnp.float32).reshape(TILES, TILE, HEAD_DIM)
    value_tiles = value_unit.astype(jnp.float32).reshape(TILES, TILE, HEAD_DIM)
    query_blocks = query_unit.astype(jnp.float32).reshape(TILES // 8, 8, TILE, HEAD_DIM)
    key_table = pair_keys.reshape(TILES // 8, 8, KMAX)

    def one_block(packed):
        query_block, key_index = packed
        clipped = jnp.maximum(key_index, 0)
        scores = block_scores(query_block, key_tiles[clipped], key_index)
        row_max = jnp.max(scores, axis=(2, 3), keepdims=True)
        log_total = row_max + jnp.log(jnp.sum(jnp.exp(scores - row_max), axis=(2, 3), keepdims=True))
        weights = rounded(jnp.exp(scores - log_total))
        result = jnp.einsum("qakb,qkbd->qad", weights, value_tiles[clipped])
        return result.astype(jnp.bfloat16), log_total[:, :, 0, 0]

    unit_outs, unit_sums = lax.map(one_block, (query_blocks, key_table))
    return unit_outs.reshape(TOKENS, HEAD_DIM), unit_sums.reshape(TOKENS)


def unit_backward(query_unit, key_unit, value_unit, out_unit, log_unit, grad_unit, pair_keys):
    score_scale = HEAD_DIM ** -0.5
    grad_float = grad_unit.astype(jnp.float32)
    row_delta = jnp.sum(grad_float * out_unit.astype(jnp.float32), axis=-1)
    key_tiles = key_unit.astype(jnp.float32).reshape(TILES, TILE, HEAD_DIM)
    value_tiles = value_unit.astype(jnp.float32).reshape(TILES, TILE, HEAD_DIM)
    blocks = TILES // 8
    packed = (query_unit.astype(jnp.float32).reshape(blocks, 8, TILE, HEAD_DIM),
              grad_float.reshape(blocks, 8, TILE, HEAD_DIM),
              row_delta.reshape(blocks, 8, TILE),
              log_unit.reshape(blocks, 8, TILE),
              pair_keys.reshape(blocks, 8, KMAX))

    def one_block(carry, inputs):
        key_acc, value_acc = carry
        query_block, grad_block, delta_block, log_block, key_index = inputs
        clipped = jnp.maximum(key_index, 0)
        key_block = key_tiles[clipped]
        value_block = value_tiles[clipped]
        scores = block_scores(query_block, key_block, key_index)
        prob_full = jnp.exp(scores - log_block[:, :, None, None])
        weights = rounded(prob_full)
        value_part = jnp.einsum("qakb,qad->qkbd", weights, grad_block)
        grad_probs = jnp.einsum("qad,qkbd->qakb", grad_block, value_block)
        grad_scores = rounded(prob_full * (grad_probs - delta_block[:, :, None, None]) * score_scale)
        query_grad = jnp.einsum("qakb,qkbd->qad", grad_scores, key_block).astype(jnp.bfloat16)
        key_part = jnp.einsum("qakb,qad->qkbd", grad_scores, query_block)
        key_acc = key_acc.at[clipped].add(key_part)
        value_acc = value_acc.at[clipped].add(value_part)
        return (key_acc, value_acc), query_grad

    empty_acc = jnp.zeros((TILES, TILE, HEAD_DIM), jnp.float32)
    (key_acc, value_acc), query_grads = lax.scan(one_block, (empty_acc, empty_acc), packed)
    return (query_grads.reshape(TOKENS, HEAD_DIM),
            key_acc.reshape(TOKENS, HEAD_DIM).astype(jnp.bfloat16),
            value_acc.reshape(TOKENS, HEAD_DIM).astype(jnp.bfloat16))


def to_units(values):
    return jnp.transpose(values, (1, 2, 0, 3)).reshape(VIDEOS * HEADS, TOKENS, HEAD_DIM)


def from_units(values):
    return jnp.transpose(values.reshape(VIDEOS, HEADS, TOKENS, HEAD_DIM), (2, 0, 1, 3))


def reference(queries, keys_in, values_in, pair_keys, out_weight, cotangent):
    query_units = to_units(queries)
    key_units = to_units(keys_in)
    value_units = to_units(values_in)
    out_units, log_units = lax.map(lambda packed: unit_forward(packed[0], packed[1], packed[2], pair_keys),
                                   (query_units, key_units, value_units))
    attention = from_units(out_units).reshape(TOKENS * VIDEOS, HEADS * HEAD_DIM)
    cot_rows = cotangent.reshape(TOKENS * VIDEOS, D)
    output = jnp.dot(attention, out_weight, preferred_element_type=jnp.float32).astype(jnp.bfloat16)
    weight_grad = jnp.dot(attention.T, cot_rows, preferred_element_type=jnp.float32)
    grad_attention = jnp.dot(cot_rows, out_weight.T, preferred_element_type=jnp.float32).astype(jnp.bfloat16)
    grad_units = to_units(grad_attention.reshape(TOKENS, VIDEOS, HEADS, HEAD_DIM))
    grad_q, grad_k, grad_v = lax.map(
        lambda packed: unit_backward(packed[0], packed[1], packed[2], packed[3], packed[4], packed[5], pair_keys),
        (query_units, key_units, value_units, out_units, log_units, grad_units))
    return (output.reshape(TOKENS, VIDEOS, D), from_units(grad_q), from_units(grad_k),
            from_units(grad_v), weight_grad)
```

```python
import functools

import jax
import jax.numpy as jnp
from jax import lax
from jax.experimental import pallas as pl
from jax.experimental.pallas import tpu as pltpu
from jax.sharding import PartitionSpec as P

F32, BF16 = jnp.float32, jnp.bfloat16
TILE = 64
SIDE = 4
ROW = SIDE * TILE
LOG2E = 1.4426950408889634
VMEM_BYTES = 60 * 1024 * 1024
NT = (((1,), (1,)), ((), ()))
NN = (((1,), (0,)), ((), ()))


def dot(a, b, dims=NN):
    return lax.dot_general(a, b, dims, preferred_element_type=F32)


def order_kernel(pairs_ref, order_ref):
    pairs = pairs_ref[...]
    tiles, slots = pairs.shape
    lane = lax.broadcasted_iota(jnp.int32, (tiles, tiles), 1)
    line = lax.broadcasted_iota(jnp.int32, (tiles, tiles), 0)
    near = jnp.zeros((tiles, tiles), F32)
    for slot in range(slots):
        near += (pairs[:, slot : slot + 1] == lane).astype(F32)
    near_b = near.astype(BF16)
    walks = dot(dot(near_b, near_b).astype(BF16), near_b)
    corner = jnp.sum(near, axis=0, keepdims=True) == 8.0
    ids = lane[:1]

    def first(mask):
        return jnp.min(jnp.where(mask, ids, tiles), axis=1, keepdims=True)

    def walks_from(tile):
        return jnp.sum(jnp.where(line == tile, walks, 0.0), axis=0, keepdims=True)

    base = walks_from(first(corner))
    ends = corner & (base == 16.0)
    place = jnp.zeros((1, tiles), jnp.int32)
    for _ in range(3):
        end = first(ends)
        ends = ends & (ids != end)
        far = walks_from(end)
        step = (
            (5.0 * far >= 3.0 * base).astype(jnp.int32)
            + (3.0 * far >= 5.0 * base).astype(jnp.int32)
            + (far >= 4.0 * base).astype(jnp.int32)
        )
        place = SIDE * place + step
    order_ref[...] = jnp.sum(jnp.where(place == line, lane, 0), axis=1, keepdims=True)


def grid_order(pair_keys):
    tiles = pair_keys.shape[0]
    return pl.pallas_call(
        order_kernel, out_shape=jax.ShapeDtypeStruct((tiles, 1), jnp.int32), name="grid_order"
    )(pair_keys).reshape(tiles)


def move_tiles(order_ref, remote, arrays, sem, inbound):
    @pl.loop(0, order_ref.shape[0])
    def _(place):
        tile = order_ref[place]
        far = remote.at[tile // 2, :, pl.ds(pl.multiple_of((tile % 2) * TILE, TILE), TILE)]
        here = arrays.at[:, pl.ds(pl.multiple_of(place * TILE, TILE), TILE)]
        if inbound:
            pltpu.make_async_copy(far, here, sem).start()
        else:
            pltpu.make_async_copy(here, far, sem).start()


def await_tiles(arrays, sem):
    pltpu.make_async_copy(arrays, arrays, sem).wait()


def transposed(source, target):
    for block in range(source.shape[0] // ROW):
        rows = pl.ds(block * ROW, ROW)
        target[:, rows] = source[rows, :].T


def window(r):
    low, high = max(r - 1, 0), min(r + 1, SIDE - 1)
    return low, high - low + 1


STARTS = [sum(window(i)[1] for i in range(r)) for r in range(SIDE + 1)]
LEFT = (slice(0, 3 * TILE), slice(0, 2 * TILE))
RIGHT = (slice(TILE, 4 * TILE), slice(2 * TILE, 4 * TILE))


def masked(scores, b):
    block = scores[b * ROW : (b + 1) * ROW]
    left, right = block[LEFT], block[RIGHT]
    first = lax.broadcasted_iota(jnp.int32, (TILE, 2 * TILE), 1) < TILE
    left = jnp.concatenate([left[: 2 * TILE], jnp.where(first, -jnp.inf, left[2 * TILE :])], axis=0)
    right = jnp.concatenate([jnp.where(first, right[:TILE], -jnp.inf), right[TILE:]], axis=0)
    return left, right


def sides(row):
    return row[:, : 2 * TILE], row[:, 2 * TILE :]


def rows_of(frame, r, count=1):
    return pl.ds(pl.multiple_of((frame * SIDE + r) * ROW, ROW), count * ROW)


def frames_near(frame):
    return jnp.maximum(frame - 1, 0), jnp.minimum(frame + 2, SIDE)


def forward_kernel(
    scale, order_ref, recv_ref, out_ref, grid_ref, log_ref,
    kvq_v, vt_v, weights_v, top_v, total_v, acc_v, in_sem, out_sem,
):
    move_tiles(order_ref, recv_ref, kvq_v, in_sem, True)
    weights_v[...] = jnp.zeros_like(weights_v)
    await_tiles(kvq_v, in_sem)
    transposed(kvq_v.at[1], vt_v)
    factor = scale * LOG2E

    @pl.loop(0, SIDE)
    def _(frame):
        top_v[...] = jnp.full_like(top_v, -jnp.inf)
        total_v[...] = jnp.zeros_like(total_v)
        acc_v[...] = jnp.zeros_like(acc_v)

        @pl.loop(*frames_near(frame))
        def _(other):
            def score(r):
                low, count = window(r)
                return dot(kvq_v[0, rows_of(other, low, count)], kvq_v[2, rows_of(frame, r)], NT)

            def weigh(r, scores):
                low, count = window(r)
                parts = [masked(scores, b) for b in range(count)]
                top = top_v[r : r + 1]
                highest = [
                    functools.reduce(
                        jnp.maximum, [jnp.max(p[side], axis=0, keepdims=True) for p in parts]
                    )
                    for side in range(2)
                ]
                new_top = jnp.maximum(top, jnp.concatenate(highest, axis=1) * factor)
                fade = jnp.exp2(top - new_top)
                tops = sides(new_top)
                sums = [0.0, 0.0]
                for b, p in enumerate(parts):
                    for side, where in enumerate((LEFT, RIGHT)):
                        e = jnp.exp2(p[side] * factor - tops[side])
                        sums[side] += jnp.sum(e, axis=0, keepdims=True)
                        weights_v[(STARTS[r] + b,) + where] = e.astype(BF16)
                total_v[r : r + 1] = total_v[r : r + 1] * fade + jnp.concatenate(sums, axis=1)
                top_v[r : r + 1] = new_top
                weights = weights_v[STARTS[r] : STARTS[r + 1]].reshape(count * ROW, ROW)
                acc_v[r] = acc_v[r] * fade + dot(vt_v[:, rows_of(other, low, count)], weights)

            ahead = score(0)
            for r in range(SIDE):
                scores, ahead = ahead, score(r + 1) if r + 1 < SIDE else None
                weigh(r, scores)

        for r in range(SIDE):
            total = total_v[r : r + 1]
            grid_ref[0, rows_of(frame, r)] = (acc_v[r] / total).T.astype(BF16)
            log_ref[frame, r : r + 1] = top_v[r : r + 1] + jnp.log2(total)

    move_tiles(order_ref, out_ref, grid_ref, out_sem, False)
    await_tiles(grid_ref, out_sem)


def backward_kernel(
    scale, order_ref, recv_ref, grad_ref, att_ref, log_ref, out_ref,
    kvq_v, g_v, out_v, kt_v, dk_acc, dv_acc, weights_v, slopes_v, acc_v, in_sem, grad_sem, out_sem,
):
    head_size = kvq_v.shape[2]
    move_tiles(order_ref, recv_ref, kvq_v, in_sem, True)
    move_tiles(order_ref, grad_ref, g_v, grad_sem, True)
    weights_v[...] = jnp.zeros_like(weights_v)
    slopes_v[...] = jnp.zeros_like(slopes_v)
    dk_acc[...] = jnp.zeros_like(dk_acc)
    dv_acc[...] = jnp.zeros_like(dv_acc)
    await_tiles(kvq_v, in_sem)
    transposed(kvq_v.at[0], kt_v)
    await_tiles(g_v, grad_sem)
    factor = scale * LOG2E
    ones = jnp.ones((8, head_size), BF16)

    @pl.loop(0, SIDE)
    def _(frame):
        acc_v[...] = jnp.zeros_like(acc_v)
        deltas, logs = [], []
        for r in range(SIDE):
            rows = rows_of(frame, r)
            product = g_v[0, rows].astype(F32) * att_ref[0, rows].astype(F32)
            upper = product.astype(BF16)
            lower = (product - upper.astype(F32)).astype(BF16)
            deltas.append(sides((dot(ones, upper, NT) + dot(ones, lower, NT))[:1]))
            logs.append(sides(log_ref[frame, r : r + 1]))

        @pl.loop(*frames_near(frame))
        def _(other):
            def score(r):
                low, count = window(r)
                keys = rows_of(other, low, count)
                rows = rows_of(frame, r)
                return (
                    dot(kvq_v[0, keys], kvq_v[2, rows], NT),
                    dot(kvq_v[1, keys], g_v[0, rows], NT),
                )

            def weigh(r, scores, grad_probs):
                low, count = window(r)
                for b in range(count):
                    parts = masked(scores, b)
                    block = grad_probs[b * ROW : (b + 1) * ROW]
                    for side, where in enumerate((LEFT, RIGHT)):
                        probs = jnp.exp2(parts[side] * factor - logs[r][side])
                        slopes = probs * (block[where] - deltas[r][side])
                        weights_v[(STARTS[r] + b,) + where] = probs.astype(BF16)
                        slopes_v[(STARTS[r] + b,) + where] = slopes.astype(BF16)
                slopes = slopes_v[STARTS[r] : STARTS[r + 1]].reshape(count * ROW, ROW)
                acc_v[r] += dot(kt_v[:, rows_of(other, low, count)], slopes)

            def collect(key_r):
                low, count = window(key_r)
                picks = [STARTS[r] + key_r - window(r)[0] for r in range(low, low + count)]
                keys = rows_of(other, key_r)
                rows = rows_of(frame, low, count)
                dv_acc[keys] += dot(
                    jnp.concatenate([weights_v[b] for b in picks], axis=1), g_v[0, rows]
                )
                dk_acc[keys] += dot(
                    jnp.concatenate([slopes_v[b] for b in picks], axis=1), kvq_v[2, rows]
                )

            ahead = score(0)
            for r in range(SIDE):
                now, ahead = ahead, score(r + 1) if r + 1 < SIDE else None
                weigh(r, *now)
                if r > 0:
                    collect(r - 1)
            collect(SIDE - 1)

        for r in range(SIDE):
            out_v[2, rows_of(frame, r)] = (acc_v[r] * scale).T.astype(BF16)

    out_v[0] = (dk_acc[...] * scale).astype(BF16)
    out_v[1] = dv_acc[...].astype(BF16)
    move_tiles(order_ref, out_ref, out_v, out_sem, False)
    await_tiles(out_v, out_sem)


SMEM = pl.BlockSpec(memory_space=pltpu.SMEM)
ANYWHERE = pl.BlockSpec(memory_space=pl.ANY)
VMEM = pl.BlockSpec(memory_space=pltpu.VMEM)


def attend(order, received):
    shards, _, rows, head_size = received.shape
    tokens = shards * rows
    square = pltpu.VMEM((STARTS[SIDE], ROW, ROW), BF16)
    return pl.pallas_call(
        functools.partial(forward_kernel, head_size**-0.5),
        out_shape=(
            jax.ShapeDtypeStruct((shards, 1, rows, head_size), BF16),
            jax.ShapeDtypeStruct((1, tokens, head_size), BF16),
            jax.ShapeDtypeStruct((SIDE, SIDE, ROW), F32),
        ),
        in_specs=[SMEM, ANYWHERE],
        out_specs=(ANYWHERE, VMEM, VMEM),
        scratch_shapes=[
            pltpu.VMEM((3, tokens, head_size), BF16), pltpu.VMEM((head_size, tokens), BF16), square,
            pltpu.VMEM((SIDE, ROW), F32), pltpu.VMEM((SIDE, ROW), F32),
            pltpu.VMEM((SIDE, head_size, ROW), F32),
            pltpu.SemaphoreType.DMA, pltpu.SemaphoreType.DMA,
        ],
        compiler_params=pltpu.CompilerParams(vmem_limit_bytes=36 * 1024 * 1024),
        cost_estimate=pl.CostEstimate(
            flops=8 * 10**9, bytes_accessed=4 * tokens * head_size * 2, transcendentals=6 * 10**6
        ),
        name="attend",
    )(order, received)


def attend_back(order, received, grad, attended, log_total):
    shards, _, rows, head_size = received.shape
    tokens = shards * rows
    square = pltpu.VMEM((STARTS[SIDE], ROW, ROW), BF16)
    total = pltpu.VMEM((tokens, head_size), F32)
    return pl.pallas_call(
        functools.partial(backward_kernel, head_size**-0.5),
        out_shape=jax.ShapeDtypeStruct((shards, 3, rows, head_size), BF16),
        in_specs=[SMEM, ANYWHERE, ANYWHERE, VMEM, VMEM],
        out_specs=ANYWHERE,
        scratch_shapes=[
            pltpu.VMEM((3, tokens, head_size), BF16), pltpu.VMEM((1, tokens, head_size), BF16),
            pltpu.VMEM((3, tokens, head_size), BF16),
            pltpu.VMEM((head_size, tokens), BF16), total, total, square, square,
            pltpu.VMEM((SIDE, head_size, ROW), F32),
            pltpu.SemaphoreType.DMA, pltpu.SemaphoreType.DMA, pltpu.SemaphoreType.DMA,
        ],
        compiler_params=pltpu.CompilerParams(vmem_limit_bytes=36 * 1024 * 1024),
        cost_estimate=pl.CostEstimate(
            flops=18 * 10**9, bytes_accessed=8 * tokens * head_size * 2, transcendentals=6 * 10**6
        ),
        name="attend_back",
    )(order, received, grad, attended, log_total)


def place_weight(coords_ref, near, far, weight_v, sem):
    width = near[0].shape[2]
    for other, pieces in enumerate((near, far)):
        for dy, piece in enumerate(pieces):
            column = pl.multiple_of(lax.rem(coords_ref[0] + dy, SIDE) * width, 128)
            half = jnp.bitwise_xor(coords_ref[1], other)
            pltpu.make_async_copy(
                piece, weight_v.at[:, half, :, pl.ds(column, width)], sem
            ).start()


def project_back_kernel(coords_ref, cot_ref, *refs):
    near, far = refs[:SIDE], refs[SIDE : 2 * SIDE]
    first_ref, out_ref, weight_v, sem = refs[2 * SIDE :]
    place_weight(coords_ref, near, far, weight_v, sem)
    pltpu.make_async_copy(weight_v, weight_v, sem).wait()
    heads = out_ref.shape[0] // 2
    rows, size = out_ref.shape[2:]
    for pair in range(heads // 2):
        grads = dot(
            cot_ref[...], weight_v[4 * pair : 4 * pair + 4].reshape(2 * size, -1), NT
        ).astype(BF16)
        for video in range(2):
            for one in range(2):
                out_ref[video * heads + pair * 2 + one, 0] = grads[
                    video * rows : (video + 1) * rows, one * size : (one + 1) * size
                ]


def weight_grad_kernel(coords_ref, att_ref, cot_ref, first_ref, keep_ref, send_ref):
    y, core = coords_ref[0], coords_ref[1]
    heads = att_ref.shape[0] // 2
    width = keep_ref.shape[2]
    cot = cot_ref[...]
    mine = jnp.broadcast_to(core == 0, (TILE, cot.shape[1]))
    for head in range(heads):
        both = jnp.concatenate([att_ref[head, 0], att_ref[heads + head, 0]], axis=0)
        part = lax.dot_general(both, cot, (((0,), (0,)), ((), ())), preferred_element_type=F32)
        keep = jnp.where(mine, part[:TILE], part[TILE:]).astype(BF16)
        send = jnp.where(mine, part[TILE:], part[:TILE]).astype(BF16)
        line = slice(head * TILE, (head + 1) * TILE)
        for block in range(SIDE):
            dy = lax.rem(block - y + SIDE, SIDE)
            columns = slice(block * width, (block + 1) * width)
            keep_ref[dy, line] = keep[:, columns]
            send_ref[dy, line] = send[:, columns]


def output_kernel(coords_ref, att_ref, *refs):
    near, far = refs[:SIDE], refs[SIDE : 2 * SIDE]
    first_ref, out_ref, weight_v, att_v, sem = refs[2 * SIDE :]
    place_weight(coords_ref, near, far, weight_v, sem)
    heads = att_ref.shape[0] // 2
    rows, size = att_ref.shape[2:]
    for head in range(heads):
        for video in range(2):
            att_v[video * rows : (video + 1) * rows, head * size : (head + 1) * size] = att_ref[
                video * heads + head, 0
            ]
    pltpu.make_async_copy(weight_v, weight_v, sem).wait()
    weight = weight_v[...].reshape(att_v.shape[1], -1)
    out_ref[...] = dot(att_v[...], weight).astype(BF16)


def project_back(coords, cot_rows, near, far, heads, size, first):
    rows, columns = cot_rows.shape
    units = 2 * heads
    return pl.pallas_call(
        project_back_kernel,
        out_shape=jax.ShapeDtypeStruct((2 * heads, 1, rows // 2, size), BF16),
        in_specs=[SMEM, VMEM] + [ANYWHERE] * (2 * SIDE + 1),
        out_specs=VMEM,
        scratch_shapes=[pltpu.VMEM((units, 2, TILE // 2, columns), BF16), pltpu.SemaphoreType.DMA],
        compiler_params=pltpu.CompilerParams(vmem_limit_bytes=VMEM_BYTES),
        cost_estimate=pl.CostEstimate(
            flops=2 * rows * columns * heads * size, bytes_accessed=9 * 10**6, transcendentals=0
        ),
        name="project_back",
    )(coords, cot_rows, *near, *far, first)


def weight_grad_parts(coords, attended, cot_rows, width, first):
    units, _, _, size = attended.shape
    rows, columns = cot_rows.shape
    half = jax.ShapeDtypeStruct((SIDE, units * size // 4, width), BF16)
    return pl.pallas_call(
        weight_grad_kernel,
        out_shape=(half, half),
        in_specs=[SMEM, VMEM, VMEM, ANYWHERE],
        out_specs=(VMEM, VMEM),
        compiler_params=pltpu.CompilerParams(vmem_limit_bytes=40 * 1024 * 1024),
        cost_estimate=pl.CostEstimate(
            flops=rows * columns * units * size, bytes_accessed=8 * 10**6, transcendentals=0
        ),
        name="weight_grad_parts",
    )(coords, attended, cot_rows, first)


def project(coords, attended, columns, near, far, first):
    units, _, depth, size = attended.shape
    rows, heads = 2 * depth, units // 2
    return pl.pallas_call(
        output_kernel,
        out_shape=jax.ShapeDtypeStruct((rows, columns), BF16),
        in_specs=[SMEM, VMEM] + [ANYWHERE] * (2 * SIDE + 1),
        out_specs=VMEM,
        scratch_shapes=[
            pltpu.VMEM((units, 2, TILE // 2, columns), BF16), pltpu.VMEM((rows, heads * size), BF16),
            pltpu.SemaphoreType.DMA,
        ],
        compiler_params=pltpu.CompilerParams(vmem_limit_bytes=40 * 1024 * 1024),
        cost_estimate=pl.CostEstimate(
            flops=2 * rows * columns * heads * size, bytes_accessed=8 * 10**6, transcendentals=0
        ),
        name="project",
    )(coords, attended, *near, *far, first)


def along_y(array, step):
    return lax.ppermute(array, "dp", [(i, (i + step) % SIDE) for i in range(SIDE)])


def to_other_core(array):
    return lax.ppermute(array, "seq", [(i, i ^ 1) for i in range(lax.axis_size("seq"))])


def summed(terms):
    return functools.reduce(jnp.add, [t.astype(F32) for t in terms])


def scatter_near(keep, send):
    total = summed([keep, to_other_core(send)]).astype(BF16)
    return summed([total[0]] + [along_y(total[d], d) for d in range(1, SIDE)]).astype(BF16)


def scatter_far(total):
    shards = lax.axis_size("seq")
    total = lax.all_to_all(
        total.reshape(shards // 2, TILE, -1), "seq", split_axis=0, concat_axis=0, tiled=True,
        axis_index_groups=[list(range(core, shards, 2)) for core in range(2)],
    )
    return jnp.sum(total.astype(F32), axis=0)


def gather_weight(block):
    shards = lax.axis_size("seq")
    depth, width = block.shape
    sent = jnp.broadcast_to(
        block.reshape(1, 2, depth // 2, width), (shards // 2, 2, depth // 2, width)
    )
    return exchange(sent.reshape(shards, depth // 2, width))


def pack_kernel(*refs):
    out_ref = refs[-1]
    for index, ref in enumerate(refs[:-1]):
        out_ref[:, index] = jnp.swapaxes(ref[...], 0, 1)


def pack(arrays):
    tokens, units, size = arrays[0].shape
    step = tokens // 4
    return pl.pallas_call(
        pack_kernel,
        grid=(4,),
        out_shape=jax.ShapeDtypeStruct((units, len(arrays), tokens, size), BF16),
        in_specs=[pl.BlockSpec((step, units, size), lambda i: (i, 0, 0))] * len(arrays),
        out_specs=pl.BlockSpec((units, len(arrays), step, size), lambda i: (0, 0, i, 0)),
        compiler_params=pltpu.CompilerParams(vmem_limit_bytes=VMEM_BYTES),
        name="pack",
    )(*arrays)


def unpack_kernel(in_ref, *refs):
    for index, ref in enumerate(refs):
        ref[...] = jnp.swapaxes(in_ref[:, index], 0, 1)


def unpack(array):
    units, count, tokens, size = array.shape
    step = tokens // 4
    return pl.pallas_call(
        unpack_kernel,
        grid=(4,),
        out_shape=[jax.ShapeDtypeStruct((tokens, units, size), BF16)] * count,
        in_specs=[pl.BlockSpec((units, count, step, size), lambda i: (0, 0, i, 0))],
        out_specs=[pl.BlockSpec((step, units, size), lambda i: (i, 0, 0))] * count,
        compiler_params=pltpu.CompilerParams(vmem_limit_bytes=40 * 1024 * 1024),
        name="unpack",
    )(array)


def after_kernel(array_ref, *refs):
    pass


def after(array, *first):
    return pl.pallas_call(
        after_kernel,
        out_shape=jax.ShapeDtypeStruct(array.shape, array.dtype),
        in_specs=[ANYWHERE] * (1 + len(first)),
        out_specs=ANYWHERE,
        input_output_aliases={0: 0},
        name="after",
    )(array, *first)


def exchange(array):
    return lax.all_to_all(array, "seq", split_axis=0, concat_axis=0, tiled=True)


def local(queries, keys_in, values_in, pair_keys, out_weight, cotangent):
    rows, videos, heads, head_size = queries.shape
    columns = cotangent.shape[2]
    coords = jnp.stack([lax.axis_index("dp"), lax.axis_index("seq") % 2]).astype(jnp.int32)
    units = videos * heads
    order = grid_order(pair_keys)
    cot_rows = jnp.transpose(cotangent, (1, 0, 2)).reshape(videos * rows, columns)
    packed = pack([a.reshape(rows, units, head_size) for a in (keys_in, values_in, queries)])
    block = gather_weight(out_weight)
    received = exchange(after(packed, block, order, cot_rows))
    near = [block] + [along_y(block, -d) for d in range(1, SIDE)]
    far = [to_other_core(piece) for piece in near]
    grad_sent = project_back(coords, cot_rows, near, far, heads, head_size, order)
    grad_received = exchange(grad_sent)
    received = after(received, grad_sent)
    attended, attended_grid, log_total = attend(order, received)
    attended_tok = exchange(attended)
    grads_sent = attend_back(order, received, grad_received, attended_grid, log_total)
    total = scatter_near(
        *weight_grad_parts(coords, attended_tok, cot_rows, out_weight.shape[1], grads_sent)
    )
    output = project(coords, attended_tok, columns, near, far, total)
    output = jnp.transpose(output.reshape(videos, rows, columns), (1, 0, 2))
    grad_k, grad_v, grad_q = (a.reshape(queries.shape) for a in unpack(exchange(grads_sent)))
    return output, grad_q, grad_k, grad_v, scatter_far(total)


def solution(mesh):
    placed = (
        P("seq", "dp", None, None),
        P("seq", "dp", None, None),
        P("seq", "dp", None, None),
        P(),
        P("seq", "dp"),
        P("seq", "dp", None),
    )
    return jax.shard_map(
        local,
        mesh=mesh,
        in_specs=placed,
        out_specs=(
            P("seq", "dp", None),
            P("seq", "dp", None, None),
            P("seq", "dp", None, None),
            P("seq", "dp", None, None),
            P("seq", "dp"),
        ),
        check_vma=False,
    )
```

```python
import functools

import jax
import jax.numpy as jnp
from jax import lax
from jax.experimental import pallas as pl
from jax.experimental.pallas import tpu as pltpu
from jax.sharding import PartitionSpec as P

F32, BF16 = jnp.float32, jnp.bfloat16
TILE = 64
SIDE = 4
ROW = SIDE * TILE
LOG2E = 1.4426950408889634
VMEM_BYTES = 60 * 1024 * 1024
NT = (((1,), (1,)), ((), ()))
NN = (((1,), (0,)), ((), ()))


def dot(a, b, dims=NN):
    return lax.dot_general(a, b, dims, preferred_element_type=F32)


def order_kernel(pairs_ref, order_ref):
    pairs = pairs_ref[...]
    tiles, slots = pairs.shape
    lane = lax.broadcasted_iota(jnp.int32, (tiles, tiles), 1)
    line = lax.broadcasted_iota(jnp.int32, (tiles, tiles), 0)
    near = jnp.zeros((tiles, tiles), F32)
    for slot in range(slots):
        near += (pairs[:, slot : slot + 1] == lane).astype(F32)
    near_b = near.astype(BF16)
    walks = dot(dot(near_b, near_b).astype(BF16), near_b)
    corner = jnp.sum(near, axis=0, keepdims=True) == 8.0
    ids = lane[:1]

    def first(mask):
        return jnp.min(jnp.where(mask, ids, tiles), axis=1, keepdims=True)

    def walks_from(tile):
        return jnp.sum(jnp.where(line == tile, walks, 0.0), axis=0, keepdims=True)

    base = walks_from(first(corner))
    ends = corner & (base == 16.0)
    place = jnp.zeros((1, tiles), jnp.int32)
    for _ in range(3):
        end = first(ends)
        ends = ends & (ids != end)
        far = walks_from(end)
        step = (
            (5.0 * far >= 3.0 * base).astype(jnp.int32)
            + (3.0 * far >= 5.0 * base).astype(jnp.int32)
            + (far >= 4.0 * base).astype(jnp.int32)
        )
        place = SIDE * place + step
    order_ref[...] = jnp.sum(jnp.where(place == line, lane, 0), axis=1, keepdims=True)


def grid_order(pair_keys):
    tiles = pair_keys.shape[0]
    return pl.pallas_call(
        order_kernel, out_shape=jax.ShapeDtypeStruct((tiles, 1), jnp.int32), name="grid_order"
    )(pair_keys).reshape(tiles)


def move_tiles(order_ref, remote, arrays, sem, inbound):
    @pl.loop(0, order_ref.shape[0])
    def _(place):
        tile = order_ref[place]
        far = remote.at[tile // 2, :, pl.ds(pl.multiple_of((tile % 2) * TILE, TILE), TILE)]
        here = arrays.at[:, pl.ds(pl.multiple_of(place * TILE, TILE), TILE)]
        if inbound:
            pltpu.make_async_copy(far, here, sem).start()
        else:
            pltpu.make_async_copy(here, far, sem).start()


def await_tiles(arrays, sem):
    pltpu.make_async_copy(arrays, arrays, sem).wait()


def transposed(source, target):
    for block in range(source.shape[0] // ROW):
        rows = pl.ds(block * ROW, ROW)
        target[:, rows] = source[rows, :].T


def window(r):
    low, high = max(r - 1, 0), min(r + 1, SIDE - 1)
    return low, high - low + 1


STARTS = [sum(window(i)[1] for i in range(r)) for r in range(SIDE + 1)]
LEFT = (slice(0, 3 * TILE), slice(0, 2 * TILE))
RIGHT = (slice(TILE, 4 * TILE), slice(2 * TILE, 4 * TILE))


def masked(scores, b):
    block = scores[b * ROW : (b + 1) * ROW]
    left, right = block[LEFT], block[RIGHT]
    first = lax.broadcasted_iota(jnp.int32, (TILE, 2 * TILE), 1) < TILE
    left = jnp.concatenate([left[: 2 * TILE], jnp.where(first, -jnp.inf, left[2 * TILE :])], axis=0)
    right = jnp.concatenate([jnp.where(first, right[:TILE], -jnp.inf), right[TILE:]], axis=0)
    return left, right


def sides(row):
    return row[:, : 2 * TILE], row[:, 2 * TILE :]


def rows_of(frame, r, count=1):
    return pl.ds((frame * SIDE + r) * ROW, count * ROW)


def frames_near(frame):
    return range(max(frame - 1, 0), min(frame + 2, SIDE))


def forward_kernel(
    scale, order_ref, recv_ref, token_ref, out_ref, grid_ref, log_ref,
    kvq_v, vt_v, weights_v, top_v, total_v, acc_v, in_sem, out_sem,
):
    move_tiles(order_ref, recv_ref, kvq_v, in_sem, True)
    weights_v[...] = jnp.zeros_like(weights_v)
    await_tiles(kvq_v, in_sem)
    transposed(kvq_v.at[1], vt_v)
    factor = scale * LOG2E

    for frame in range(SIDE):
        top_v[...] = jnp.full_like(top_v, -jnp.inf)
        total_v[...] = jnp.zeros_like(total_v)
        acc_v[...] = jnp.zeros_like(acc_v)

        for other in frames_near(frame):
            def score(r):
                low, count = window(r)
                return dot(kvq_v[0, rows_of(other, low, count)], kvq_v[2, rows_of(frame, r)], NT)

            def weigh(r, scores):
                low, count = window(r)
                parts = [masked(scores, b) for b in range(count)]
                top = top_v[r : r + 1]
                highest = [
                    functools.reduce(
                        jnp.maximum, [jnp.max(p[side], axis=0, keepdims=True) for p in parts]
                    )
                    for side in range(2)
                ]
                new_top = jnp.maximum(top, jnp.concatenate(highest, axis=1) * factor)
                fade = jnp.exp2(top - new_top)
                tops = sides(new_top)
                sums = [0.0, 0.0]
                for b, p in enumerate(parts):
                    for side, where in enumerate((LEFT, RIGHT)):
                        e = jnp.exp2(p[side] * factor - tops[side])
                        sums[side] += jnp.sum(e, axis=0, keepdims=True)
                        weights_v[(STARTS[r] + b,) + where] = e.astype(BF16)
                total_v[r : r + 1] = total_v[r : r + 1] * fade + jnp.concatenate(sums, axis=1)
                top_v[r : r + 1] = new_top
                weights = weights_v[STARTS[r] : STARTS[r + 1]].reshape(count * ROW, ROW)
                acc_v[r] = acc_v[r] * fade + dot(vt_v[:, rows_of(other, low, count)], weights)

            ahead = score(0)
            for r in range(SIDE):
                scores, ahead = ahead, score(r + 1) if r + 1 < SIDE else None
                weigh(r, scores)

        for r in range(SIDE):
            total = total_v[r : r + 1]
            grid_ref[0, rows_of(frame, r)] = (acc_v[r] / total).T.astype(BF16)
            log_ref[frame, r : r + 1] = top_v[r : r + 1] + jnp.log2(total)

    move_tiles(order_ref, out_ref, grid_ref, out_sem, False)
    await_tiles(grid_ref, out_sem)


def backward_kernel(
    scale, order_ref, recv_ref, grad_ref, att_ref, log_ref, out_ref, token_ref,
    kvq_v, g_v, out_v, kt_v, dk_acc, dv_acc, weights_v, slopes_v, acc_v, in_sem, grad_sem, out_sem,
):
    head_size = kvq_v.shape[2]
    move_tiles(order_ref, recv_ref, kvq_v, in_sem, True)
    move_tiles(order_ref, grad_ref, g_v, grad_sem, True)
    weights_v[...] = jnp.zeros_like(weights_v)
    slopes_v[...] = jnp.zeros_like(slopes_v)
    dk_acc[...] = jnp.zeros_like(dk_acc)
    dv_acc[...] = jnp.zeros_like(dv_acc)
    await_tiles(kvq_v, in_sem)
    transposed(kvq_v.at[0], kt_v)
    await_tiles(g_v, grad_sem)
    factor = scale * LOG2E
    ones = jnp.ones((8, head_size), BF16)

    for frame in range(SIDE):
        acc_v[...] = jnp.zeros_like(acc_v)
        deltas, logs = [], []
        for r in range(SIDE):
            rows = rows_of(frame, r)
            product = g_v[0, rows].astype(F32) * att_ref[0, rows].astype(F32)
            upper = product.astype(BF16)
            lower = (product - upper.astype(F32)).astype(BF16)
            deltas.append(sides((dot(ones, upper, NT) + dot(ones, lower, NT))[:1]))
            logs.append(sides(log_ref[frame, r : r + 1]))

        for other in frames_near(frame):
            def score(r):
                low, count = window(r)
                keys = rows_of(other, low, count)
                rows = rows_of(frame, r)
                return (
                    dot(kvq_v[0, keys], kvq_v[2, rows], NT),
                    dot(kvq_v[1, keys], g_v[0, rows], NT),
                )

            def weigh(r, scores, grad_probs):
                low, count = window(r)
                for b in range(count):
                    parts = masked(scores, b)
                    block = grad_probs[b * ROW : (b + 1) * ROW]
                    for side, where in enumerate((LEFT, RIGHT)):
                        probs = jnp.exp2(parts[side] * factor - logs[r][side])
                        slopes = probs * (block[where] - deltas[r][side])
                        weights_v[(STARTS[r] + b,) + where] = probs.astype(BF16)
                        slopes_v[(STARTS[r] + b,) + where] = slopes.astype(BF16)
                slopes = slopes_v[STARTS[r] : STARTS[r + 1]].reshape(count * ROW, ROW)
                acc_v[r] += dot(kt_v[:, rows_of(other, low, count)], slopes)

            def collect(key_r):
                low, count = window(key_r)
                picks = [STARTS[r] + key_r - window(r)[0] for r in range(low, low + count)]
                keys = rows_of(other, key_r)
                rows = rows_of(frame, low, count)
                dv_acc[keys] += dot(
                    jnp.concatenate([weights_v[b] for b in picks], axis=1), g_v[0, rows]
                )
                dk_acc[keys] += dot(
                    jnp.concatenate([slopes_v[b] for b in picks], axis=1), kvq_v[2, rows]
                )

            ahead = score(0)
            for r in range(SIDE):
                now, ahead = ahead, score(r + 1) if r + 1 < SIDE else None
                weigh(r, *now)
                if r > 0:
                    collect(r - 1)
            collect(SIDE - 1)

        for r in range(SIDE):
            out_v[2, rows_of(frame, r)] = (acc_v[r] * scale).T.astype(BF16)

    out_v[0] = (dk_acc[...] * scale).astype(BF16)
    out_v[1] = dv_acc[...].astype(BF16)
    token_ref[...] = jnp.zeros_like(token_ref)
    move_tiles(order_ref, out_ref, out_v, out_sem, False)
    await_tiles(out_v, out_sem)


SMEM = pl.BlockSpec(memory_space=pltpu.SMEM)
ANYWHERE = pl.BlockSpec(memory_space=pl.ANY)
VMEM = pl.BlockSpec(memory_space=pltpu.VMEM)
TOKEN = jax.ShapeDtypeStruct((8, 128), F32)


def attend(order, received, token):
    shards, _, rows, head_size = received.shape
    tokens = shards * rows
    square = pltpu.VMEM((STARTS[SIDE], ROW, ROW), BF16)
    return pl.pallas_call(
        functools.partial(forward_kernel, head_size**-0.5),
        out_shape=(
            jax.ShapeDtypeStruct((shards, 1, rows, head_size), BF16),
            jax.ShapeDtypeStruct((1, tokens, head_size), BF16),
            jax.ShapeDtypeStruct((SIDE, SIDE, ROW), F32),
        ),
        in_specs=[SMEM, ANYWHERE, VMEM],
        out_specs=(ANYWHERE, VMEM, VMEM),
        scratch_shapes=[
            pltpu.VMEM((3, tokens, head_size), BF16), pltpu.VMEM((head_size, tokens), BF16), square,
            pltpu.VMEM((SIDE, ROW), F32), pltpu.VMEM((SIDE, ROW), F32),
            pltpu.VMEM((SIDE, head_size, ROW), F32),
            pltpu.SemaphoreType.DMA, pltpu.SemaphoreType.DMA,
        ],
        compiler_params=pltpu.CompilerParams(vmem_limit_bytes=VMEM_BYTES),
        cost_estimate=pl.CostEstimate(
            flops=8 * 10**9, bytes_accessed=4 * tokens * head_size * 2, transcendentals=6 * 10**6
        ),
        name="attend",
    )(order, received, token)


def attend_back(order, received, grad, attended, log_total):
    shards, _, rows, head_size = received.shape
    tokens = shards * rows
    square = pltpu.VMEM((STARTS[SIDE], ROW, ROW), BF16)
    total = pltpu.VMEM((tokens, head_size), F32)
    return pl.pallas_call(
        functools.partial(backward_kernel, head_size**-0.5),
        out_shape=(jax.ShapeDtypeStruct((shards, 3, rows, head_size), BF16), TOKEN),
        in_specs=[SMEM, ANYWHERE, ANYWHERE, VMEM, VMEM],
        out_specs=(ANYWHERE, VMEM),
        scratch_shapes=[
            pltpu.VMEM((3, tokens, head_size), BF16), pltpu.VMEM((1, tokens, head_size), BF16),
            pltpu.VMEM((3, tokens, head_size), BF16),
            pltpu.VMEM((head_size, tokens), BF16), total, total, square, square,
            pltpu.VMEM((SIDE, head_size, ROW), F32),
            pltpu.SemaphoreType.DMA, pltpu.SemaphoreType.DMA, pltpu.SemaphoreType.DMA,
        ],
        compiler_params=pltpu.CompilerParams(vmem_limit_bytes=VMEM_BYTES),
        cost_estimate=pl.CostEstimate(
            flops=18 * 10**9, bytes_accessed=8 * tokens * head_size * 2, transcendentals=6 * 10**6
        ),
        name="attend_back",
    )(order, received, grad, attended, log_total)


def place_weight(coords_ref, near, far, weight_v, sem):
    width = near[0].shape[2]
    for other, pieces in enumerate((near, far)):
        for dy, piece in enumerate(pieces):
            column = pl.multiple_of(lax.rem(coords_ref[0] + dy, SIDE) * width, 128)
            half = jnp.bitwise_xor(coords_ref[1], other)
            pltpu.make_async_copy(
                piece, weight_v.at[:, half, :, pl.ds(column, width)], sem
            ).start()


def project_back_kernel(coords_ref, cot_ref, *refs):
    near, far = refs[:SIDE], refs[SIDE : 2 * SIDE]
    out_ref, token_ref, weight_v, sem = refs[2 * SIDE :]
    place_weight(coords_ref, near, far, weight_v, sem)
    token_ref[...] = jnp.zeros_like(token_ref)
    pltpu.make_async_copy(weight_v, weight_v, sem).wait()
    heads = out_ref.shape[0] // 2
    rows, size = out_ref.shape[2:]
    for pair in range(heads // 2):
        grads = dot(
            cot_ref[...], weight_v[4 * pair : 4 * pair + 4].reshape(2 * size, -1), NT
        ).astype(BF16)
        for video in range(2):
            for one in range(2):
                out_ref[video * heads + pair * 2 + one, 0] = grads[
                    video * rows : (video + 1) * rows, one * size : (one + 1) * size
                ]


def weight_grad_kernel(coords_ref, att_ref, cot_ref, first_ref, keep_ref, send_ref):
    y, core = coords_ref[0], coords_ref[1]
    heads = att_ref.shape[0] // 2
    width = keep_ref.shape[2]
    cot = cot_ref[...]
    mine = jnp.broadcast_to(core == 0, (TILE, cot.shape[1]))
    for head in range(heads):
        both = jnp.concatenate([att_ref[head, 0], att_ref[heads + head, 0]], axis=0)
        part = lax.dot_general(both, cot, (((0,), (0,)), ((), ())), preferred_element_type=F32)
        keep = jnp.where(mine, part[:TILE], part[TILE:]).astype(BF16)
        send = jnp.where(mine, part[TILE:], part[:TILE]).astype(BF16)
        line = slice(head * TILE, (head + 1) * TILE)
        for block in range(SIDE):
            dy = lax.rem(block - y + SIDE, SIDE)
            columns = slice(block * width, (block + 1) * width)
            keep_ref[dy, line] = keep[:, columns]
            send_ref[dy, line] = send[:, columns]


def output_kernel(coords_ref, att_ref, *refs):
    near, far = refs[:SIDE], refs[SIDE : 2 * SIDE]
    first_ref, out_ref, weight_v, att_v, sem = refs[2 * SIDE :]
    place_weight(coords_ref, near, far, weight_v, sem)
    heads = att_ref.shape[0] // 2
    rows, size = att_ref.shape[2:]
    for head in range(heads):
        for video in range(2):
            att_v[video * rows : (video + 1) * rows, head * size : (head + 1) * size] = att_ref[
                video * heads + head, 0
            ]
    pltpu.make_async_copy(weight_v, weight_v, sem).wait()
    weight = weight_v[...].reshape(att_v.shape[1], -1)
    out_ref[...] = dot(att_v[...], weight).astype(BF16)


def project_back(coords, cot_rows, near, far, heads, size):
    rows, columns = cot_rows.shape
    units = 2 * heads
    return pl.pallas_call(
        project_back_kernel,
        out_shape=(jax.ShapeDtypeStruct((2 * heads, 1, rows // 2, size), BF16), TOKEN),
        in_specs=[SMEM, VMEM] + [ANYWHERE] * (2 * SIDE),
        out_specs=(VMEM, VMEM),
        scratch_shapes=[pltpu.VMEM((units, 2, TILE // 2, columns), BF16), pltpu.SemaphoreType.DMA],
        compiler_params=pltpu.CompilerParams(vmem_limit_bytes=VMEM_BYTES),
        cost_estimate=pl.CostEstimate(
            flops=2 * rows * columns * heads * size, bytes_accessed=9 * 10**6, transcendentals=0
        ),
        name="project_back",
    )(coords, cot_rows, *near, *far)


def weight_grad_parts(coords, attended, cot_rows, width, first):
    units, _, _, size = attended.shape
    rows, columns = cot_rows.shape
    half = jax.ShapeDtypeStruct((SIDE, units * size // 4, width), BF16)
    return pl.pallas_call(
        weight_grad_kernel,
        out_shape=(half, half),
        in_specs=[SMEM, VMEM, VMEM, VMEM],
        out_specs=(VMEM, VMEM),
        compiler_params=pltpu.CompilerParams(vmem_limit_bytes=VMEM_BYTES),
        cost_estimate=pl.CostEstimate(
            flops=rows * columns * units * size, bytes_accessed=8 * 10**6, transcendentals=0
        ),
        name="weight_grad_parts",
    )(coords, attended, cot_rows, first)


def project(coords, attended, columns, near, far, first):
    units, _, depth, size = attended.shape
    rows, heads = 2 * depth, units // 2
    return pl.pallas_call(
        output_kernel,
        out_shape=jax.ShapeDtypeStruct((rows, columns), BF16),
        in_specs=[SMEM, VMEM] + [ANYWHERE] * (2 * SIDE + 1),
        out_specs=VMEM,
        scratch_shapes=[
            pltpu.VMEM((units, 2, TILE // 2, columns), BF16), pltpu.VMEM((rows, heads * size), BF16),
            pltpu.SemaphoreType.DMA,
        ],
        compiler_params=pltpu.CompilerParams(vmem_limit_bytes=40 * 1024 * 1024),
        cost_estimate=pl.CostEstimate(
            flops=2 * rows * columns * heads * size, bytes_accessed=8 * 10**6, transcendentals=0
        ),
        name="project",
    )(coords, attended, *near, *far, first)


def along_y(array, step):
    return lax.ppermute(array, "dp", [(i, (i + step) % SIDE) for i in range(SIDE)])


def to_other_core(array):
    return lax.ppermute(array, "seq", [(i, i ^ 1) for i in range(lax.axis_size("seq"))])


def summed(terms):
    return functools.reduce(jnp.add, [t.astype(F32) for t in terms])


def scatter_near(keep, send):
    total = summed([keep, to_other_core(send)]).astype(BF16)
    half = total.shape[1] // 2
    passed = along_y(total[2, :half], 1), along_y(total[2, half:], -1)
    up = summed([total[1], jnp.pad(passed[0], ((0, half), (0, 0)))]).astype(BF16)
    down = summed([total[3], jnp.pad(passed[1], ((half, 0), (0, 0)))]).astype(BF16)
    return summed([total[0], along_y(up, 1), along_y(down, -1)]).astype(BF16)


def scatter_far(total):
    shards = lax.axis_size("seq")
    total = lax.all_to_all(
        total.reshape(shards // 2, TILE, -1), "seq", split_axis=0, concat_axis=0, tiled=True,
        axis_index_groups=[list(range(core, shards, 2)) for core in range(2)],
    )
    return jnp.sum(total.astype(F32), axis=0)


def gather_weight(block):
    shards = lax.axis_size("seq")
    depth, width = block.shape
    sent = jnp.broadcast_to(
        block.reshape(1, 2, depth // 2, width), (shards // 2, 2, depth // 2, width)
    )
    return exchange(sent.reshape(shards, depth // 2, width))


def pack_kernel(*refs):
    out_ref = refs[-1]
    for index, ref in enumerate(refs[:-1]):
        out_ref[:, index] = jnp.swapaxes(ref[...], 0, 1)


def pack(arrays):
    tokens, units, size = arrays[0].shape
    step = tokens // 4
    return pl.pallas_call(
        pack_kernel,
        grid=(4,),
        out_shape=jax.ShapeDtypeStruct((units, len(arrays), tokens, size), BF16),
        in_specs=[pl.BlockSpec((step, units, size), lambda i: (i, 0, 0))] * len(arrays),
        out_specs=pl.BlockSpec((units, len(arrays), step, size), lambda i: (0, 0, i, 0)),
        compiler_params=pltpu.CompilerParams(vmem_limit_bytes=VMEM_BYTES),
        name="pack",
    )(*arrays)


def unpack_kernel(in_ref, *refs):
    for index, ref in enumerate(refs):
        ref[...] = jnp.swapaxes(in_ref[:, index], 0, 1)


def unpack(array):
    units, count, tokens, size = array.shape
    step = tokens // 4
    return pl.pallas_call(
        unpack_kernel,
        grid=(4,),
        out_shape=[jax.ShapeDtypeStruct((tokens, units, size), BF16)] * count,
        in_specs=[pl.BlockSpec((units, count, step, size), lambda i: (0, 0, i, 0))],
        out_specs=[pl.BlockSpec((step, units, size), lambda i: (i, 0, 0))] * count,
        compiler_params=pltpu.CompilerParams(vmem_limit_bytes=40 * 1024 * 1024),
        name="unpack",
    )(array)


def after_kernel(array_ref, *refs):
    pass


def after(array, *first):
    return pl.pallas_call(
        after_kernel,
        out_shape=jax.ShapeDtypeStruct(array.shape, array.dtype),
        in_specs=[ANYWHERE] * (1 + len(first)),
        out_specs=ANYWHERE,
        input_output_aliases={0: 0},
        name="after",
    )(array, *first)


def exchange(array):
    return lax.all_to_all(array, "seq", split_axis=0, concat_axis=0, tiled=True)


def local(queries, keys_in, values_in, pair_keys, out_weight, cotangent):
    rows, videos, heads, head_size = queries.shape
    columns = cotangent.shape[2]
    coords = jnp.stack([lax.axis_index("dp"), lax.axis_index("seq") % 2]).astype(jnp.int32)
    units = videos * heads
    order = grid_order(pair_keys)
    cot_rows = jnp.transpose(cotangent, (1, 0, 2)).reshape(videos * rows, columns)
    packed = pack([a.reshape(rows, units, head_size) for a in (keys_in, values_in, queries)])
    block = gather_weight(out_weight)
    received = exchange(after(packed, block, order, cot_rows))
    half = block.shape[0] // 2
    up, down = along_y(block, -1), along_y(block, 1)
    opposite = jnp.concatenate([along_y(up[:half], -1), along_y(down[half:], 1)], axis=0)
    near = [block, up, opposite, down]
    far = [to_other_core(piece) for piece in near]
    grad_sent, token = project_back(coords, cot_rows, near, far, heads, head_size)
    grad_received = exchange(grad_sent)
    attended, attended_grid, log_total = attend(order, received, token)
    attended_tok = exchange(attended)
    grads_sent, token = attend_back(order, received, grad_received, attended_grid, log_total)
    total = scatter_near(
        *weight_grad_parts(coords, attended_tok, cot_rows, out_weight.shape[1], token)
    )
    output = project(coords, attended_tok, columns, near, far, total[:8])
    output = jnp.transpose(output.reshape(videos, rows, columns), (1, 0, 2))
    grad_k, grad_v, grad_q = (a.reshape(queries.shape) for a in unpack(exchange(grads_sent)))
    return output, grad_q, grad_k, grad_v, scatter_far(total)


def solution(mesh):
    placed = (
        P("seq", "dp", None, None),
        P("seq", "dp", None, None),
        P("seq", "dp", None, None),
        P(),
        P("seq", "dp"),
        P("seq", "dp", None),
    )
    return jax.shard_map(
        local,
        mesh=mesh,
        in_specs=placed,
        out_specs=(
            P("seq", "dp", None),
            P("seq", "dp", None, None),
            P("seq", "dp", None, None),
            P("seq", "dp", None, None),
            P("seq", "dp"),
        ),
        check_vma=False,
    )
```

```python
import functools

import jax
import jax.numpy as jnp
from jax import lax
from jax.experimental import pallas as pl
from jax.experimental.pallas import tpu as pltpu
from jax.sharding import PartitionSpec as P

F32, BF16 = jnp.float32, jnp.bfloat16
TILE = 64
SIDE = 4
ROW = SIDE * TILE
LOG2E = 1.4426950408889634
VMEM_BYTES = 60 * 1024 * 1024
NT = (((1,), (1,)), ((), ()))
NN = (((1,), (0,)), ((), ()))


def dot(a, b, dims=NN):
    return lax.dot_general(a, b, dims, preferred_element_type=F32)


def order_kernel(pairs_ref, order_ref):
    pairs = pairs_ref[...]
    tiles, slots = pairs.shape
    lane = lax.broadcasted_iota(jnp.int32, (tiles, tiles), 1)
    line = lax.broadcasted_iota(jnp.int32, (tiles, tiles), 0)
    near = jnp.zeros((tiles, tiles), F32)
    for slot in range(slots):
        near += (pairs[:, slot : slot + 1] == lane).astype(F32)
    near_b = near.astype(BF16)
    walks = dot(dot(near_b, near_b).astype(BF16), near_b)
    corner = jnp.sum(near, axis=0, keepdims=True) == 8.0
    ids = lane[:1]

    def first(mask):
        return jnp.min(jnp.where(mask, ids, tiles), axis=1, keepdims=True)

    def walks_from(tile):
        return jnp.sum(jnp.where(line == tile, walks, 0.0), axis=0, keepdims=True)

    base = walks_from(first(corner))
    ends = corner & (base == 16.0)
    place = jnp.zeros((1, tiles), jnp.int32)
    for _ in range(3):
        end = first(ends)
        ends = ends & (ids != end)
        far = walks_from(end)
        step = (
            (5.0 * far >= 3.0 * base).astype(jnp.int32)
            + (3.0 * far >= 5.0 * base).astype(jnp.int32)
            + (far >= 4.0 * base).astype(jnp.int32)
        )
        place = SIDE * place + step
    order_ref[...] = jnp.sum(jnp.where(place == line, lane, 0), axis=1, keepdims=True)


def grid_order(pair_keys):
    tiles = pair_keys.shape[0]
    return pl.pallas_call(
        order_kernel, out_shape=jax.ShapeDtypeStruct((tiles, 1), jnp.int32), name="grid_order"
    )(pair_keys).reshape(tiles)


def move_tiles(order_ref, remote, arrays, sem, inbound):
    @pl.loop(0, order_ref.shape[0])
    def _(place):
        tile = order_ref[place]
        far = remote.at[tile // 2, :, pl.ds(pl.multiple_of((tile % 2) * TILE, TILE), TILE)]
        here = arrays.at[:, pl.ds(pl.multiple_of(place * TILE, TILE), TILE)]
        if inbound:
            pltpu.make_async_copy(far, here, sem).start()
        else:
            pltpu.make_async_copy(here, far, sem).start()


def move_frame(order_ref, frame, remote, arrays, sem, inbound):
    for place in range(frame * SIDE * SIDE, (frame + 1) * SIDE * SIDE):
        tile = order_ref[place]
        far = remote.at[tile // 2, :, pl.ds(pl.multiple_of((tile % 2) * TILE, TILE), TILE)]
        here = arrays.at[:, place * TILE : (place + 1) * TILE]
        if inbound:
            pltpu.make_async_copy(far, here, sem).start()
        else:
            pltpu.make_async_copy(here, far, sem).start()


def await_tiles(arrays, sem):
    pltpu.make_async_copy(arrays, arrays, sem).wait()


def transposed(source, target):
    for block in range(source.shape[0] // ROW):
        rows = pl.ds(block * ROW, ROW)
        target[:, rows] = source[rows, :].T


def window(r):
    low, high = max(r - 1, 0), min(r + 1, SIDE - 1)
    return low, high - low + 1


STARTS = [sum(window(i)[1] for i in range(r)) for r in range(SIDE + 1)]
LEFT = (slice(0, 3 * TILE), slice(0, 2 * TILE))
RIGHT = (slice(TILE, 4 * TILE), slice(2 * TILE, 4 * TILE))


def masked(scores, b):
    block = scores[b * ROW : (b + 1) * ROW]
    left, right = block[LEFT], block[RIGHT]
    first = lax.broadcasted_iota(jnp.int32, (TILE, 2 * TILE), 1) < TILE
    left = jnp.concatenate([left[: 2 * TILE], jnp.where(first, -jnp.inf, left[2 * TILE :])], axis=0)
    right = jnp.concatenate([jnp.where(first, right[:TILE], -jnp.inf), right[TILE:]], axis=0)
    return left, right


def sides(row):
    return row[:, : 2 * TILE], row[:, 2 * TILE :]


def rows_of(frame, r, count=1):
    return pl.ds((frame * SIDE + r) * ROW, count * ROW)


def span(frame):
    return slice(frame * SIDE * ROW, (frame + 1) * SIDE * ROW)


def frames_near(frame):
    return range(max(frame - 1, 0), min(frame + 2, SIDE))


def forward_kernel(
    scale, order_ref, recv_ref, token_ref, out_ref, grid_ref, log_ref,
    kvq_v, vt_v, weights_v, top_v, total_v, acc_v, in_sem, out_sem,
):
    move_tiles(order_ref, recv_ref, kvq_v, in_sem, True)
    weights_v[...] = jnp.zeros_like(weights_v)
    await_tiles(kvq_v, in_sem)
    transposed(kvq_v.at[1], vt_v)
    factor = scale * LOG2E

    for frame in range(SIDE):
        top_v[...] = jnp.full_like(top_v, -jnp.inf)
        total_v[...] = jnp.zeros_like(total_v)
        acc_v[...] = jnp.zeros_like(acc_v)

        for other in frames_near(frame):
            def score(r):
                low, count = window(r)
                return dot(kvq_v[0, rows_of(other, low, count)], kvq_v[2, rows_of(frame, r)], NT)

            def weigh(r, scores):
                low, count = window(r)
                parts = [masked(scores, b) for b in range(count)]
                top = top_v[r : r + 1]
                highest = [
                    functools.reduce(
                        jnp.maximum, [jnp.max(p[side], axis=0, keepdims=True) for p in parts]
                    )
                    for side in range(2)
                ]
                new_top = jnp.maximum(top, jnp.concatenate(highest, axis=1) * factor)
                fade = jnp.exp2(top - new_top)
                tops = sides(new_top)
                sums = [0.0, 0.0]
                for b, p in enumerate(parts):
                    for side, where in enumerate((LEFT, RIGHT)):
                        e = jnp.exp2(p[side] * factor - tops[side])
                        sums[side] += jnp.sum(e, axis=0, keepdims=True)
                        weights_v[(STARTS[r] + b,) + where] = e.astype(BF16)
                total_v[r : r + 1] = total_v[r : r + 1] * fade + jnp.concatenate(sums, axis=1)
                top_v[r : r + 1] = new_top
                weights = weights_v[STARTS[r] : STARTS[r + 1]].reshape(count * ROW, ROW)
                acc_v[r] = acc_v[r] * fade + dot(vt_v[:, rows_of(other, low, count)], weights)

            ahead = score(0)
            for r in range(SIDE):
                scores, ahead = ahead, score(r + 1) if r + 1 < SIDE else None
                weigh(r, scores)

        for r in range(SIDE):
            total = total_v[r : r + 1]
            grid_ref[0, rows_of(frame, r)] = (acc_v[r] / total).T.astype(BF16)
            log_ref[frame, r : r + 1] = top_v[r : r + 1] + jnp.log2(total)

    move_tiles(order_ref, out_ref, grid_ref, out_sem, False)
    await_tiles(grid_ref, out_sem)


def backward_kernel(
    scale, order_ref, recv_ref, grad_ref, att_ref, log_ref, out_ref, token_ref,
    kvq_v, g_v, out_v, kt_v, dk_acc, dv_acc, weights_v, slopes_v, acc_v, in_sem, grad_sem, out_sem,
):
    head_size = kvq_v.shape[2]
    for frame in range(SIDE):
        move_frame(order_ref, frame, recv_ref, kvq_v, in_sem.at[frame], True)
        move_frame(order_ref, frame, grad_ref, g_v, grad_sem.at[frame], True)
    weights_v[...] = jnp.zeros_like(weights_v)
    slopes_v[...] = jnp.zeros_like(slopes_v)
    dk_acc[...] = jnp.zeros_like(dk_acc)
    dv_acc[...] = jnp.zeros_like(dv_acc)
    factor = scale * LOG2E
    ones = jnp.ones((8, head_size), BF16)

    def arrive(frame):
        rows = span(frame)
        await_tiles(kvq_v.at[:, rows], in_sem.at[frame])
        await_tiles(g_v.at[:, rows], grad_sem.at[frame])
        for r in range(SIDE):
            kt_v[:, rows_of(frame, r)] = kvq_v[0, rows_of(frame, r)].T

    def leave(frame):
        rows = span(frame)
        out_v[0, rows] = (dk_acc[rows] * scale).astype(BF16)
        out_v[1, rows] = dv_acc[rows].astype(BF16)
        move_frame(order_ref, frame, out_ref, out_v, out_sem, False)

    arrive(0)

    for frame in range(SIDE):
        acc_v[...] = jnp.zeros_like(acc_v)
        deltas, logs = [], []
        for r in range(SIDE):
            rows = rows_of(frame, r)
            product = g_v[0, rows].astype(F32) * att_ref[0, rows].astype(F32)
            upper = product.astype(BF16)
            lower = (product - upper.astype(F32)).astype(BF16)
            deltas.append(sides((dot(ones, upper, NT) + dot(ones, lower, NT))[:1]))
            logs.append(sides(log_ref[frame, r : r + 1]))

        for other in frames_near(frame):
            if other > frame:
                arrive(other)

            def score(r):
                low, count = window(r)
                keys = rows_of(other, low, count)
                rows = rows_of(frame, r)
                return (
                    dot(kvq_v[0, keys], kvq_v[2, rows], NT),
                    dot(kvq_v[1, keys], g_v[0, rows], NT),
                )

            def weigh(r, scores, grad_probs):
                low, count = window(r)
                for b in range(count):
                    parts = masked(scores, b)
                    block = grad_probs[b * ROW : (b + 1) * ROW]
                    for side, where in enumerate((LEFT, RIGHT)):
                        probs = jnp.exp2(parts[side] * factor - logs[r][side])
                        slopes = probs * (block[where] - deltas[r][side])
                        weights_v[(STARTS[r] + b,) + where] = probs.astype(BF16)
                        slopes_v[(STARTS[r] + b,) + where] = slopes.astype(BF16)
                slopes = slopes_v[STARTS[r] : STARTS[r + 1]].reshape(count * ROW, ROW)
                acc_v[r] += dot(kt_v[:, rows_of(other, low, count)], slopes)

            def collect(key_r):
                low, count = window(key_r)
                picks = [STARTS[r] + key_r - window(r)[0] for r in range(low, low + count)]
                keys = rows_of(other, key_r)
                rows = rows_of(frame, low, count)
                dv_acc[keys] += dot(
                    jnp.concatenate([weights_v[b] for b in picks], axis=1), g_v[0, rows]
                )
                dk_acc[keys] += dot(
                    jnp.concatenate([slopes_v[b] for b in picks], axis=1), kvq_v[2, rows]
                )

            ahead = score(0)
            for r in range(SIDE):
                now, ahead = ahead, score(r + 1) if r + 1 < SIDE else None
                weigh(r, *now)
                if r > 0:
                    collect(r - 1)
            collect(SIDE - 1)

        for r in range(SIDE):
            out_v[2, rows_of(frame, r)] = (acc_v[r] * scale).T.astype(BF16)

        if frame > 0:
            leave(frame - 1)
    leave(SIDE - 1)
    token_ref[...] = jnp.zeros_like(token_ref)
    await_tiles(out_v, out_sem)


SMEM = pl.BlockSpec(memory_space=pltpu.SMEM)
ANYWHERE = pl.BlockSpec(memory_space=pl.ANY)
VMEM = pl.BlockSpec(memory_space=pltpu.VMEM)
TOKEN = jax.ShapeDtypeStruct((8, 128), F32)


def attend(order, received, token):
    shards, _, rows, head_size = received.shape
    tokens = shards * rows
    square = pltpu.VMEM((STARTS[SIDE], ROW, ROW), BF16)
    return pl.pallas_call(
        functools.partial(forward_kernel, head_size**-0.5),
        out_shape=(
            jax.ShapeDtypeStruct((shards, 1, rows, head_size), BF16),
            jax.ShapeDtypeStruct((1, tokens, head_size), BF16),
            jax.ShapeDtypeStruct((SIDE, SIDE, ROW), F32),
        ),
        in_specs=[SMEM, ANYWHERE, VMEM],
        out_specs=(ANYWHERE, VMEM, VMEM),
        scratch_shapes=[
            pltpu.VMEM((3, tokens, head_size), BF16), pltpu.VMEM((head_size, tokens), BF16), square,
            pltpu.VMEM((SIDE, ROW), F32), pltpu.VMEM((SIDE, ROW), F32),
            pltpu.VMEM((SIDE, head_size, ROW), F32),
            pltpu.SemaphoreType.DMA, pltpu.SemaphoreType.DMA,
        ],
        compiler_params=pltpu.CompilerParams(vmem_limit_bytes=VMEM_BYTES),
        cost_estimate=pl.CostEstimate(
            flops=8 * 10**9, bytes_accessed=4 * tokens * head_size * 2, transcendentals=6 * 10**6
        ),
        name="attend",
    )(order, received, token)


def attend_back(order, received, grad, attended, log_total):
    shards, _, rows, head_size = received.shape
    tokens = shards * rows
    square = pltpu.VMEM((STARTS[SIDE], ROW, ROW), BF16)
    total = pltpu.VMEM((tokens, head_size), F32)
    return pl.pallas_call(
        functools.partial(backward_kernel, head_size**-0.5),
        out_shape=(jax.ShapeDtypeStruct((shards, 3, rows, head_size), BF16), TOKEN),
        in_specs=[SMEM, ANYWHERE, ANYWHERE, VMEM, VMEM],
        out_specs=(ANYWHERE, VMEM),
        scratch_shapes=[
            pltpu.VMEM((3, tokens, head_size), BF16), pltpu.VMEM((1, tokens, head_size), BF16),
            pltpu.VMEM((3, tokens, head_size), BF16),
            pltpu.VMEM((head_size, tokens), BF16), total, total, square, square,
            pltpu.VMEM((SIDE, head_size, ROW), F32),
            pltpu.SemaphoreType.DMA((SIDE,)), pltpu.SemaphoreType.DMA((SIDE,)), pltpu.SemaphoreType.DMA,
        ],
        compiler_params=pltpu.CompilerParams(vmem_limit_bytes=VMEM_BYTES),
        cost_estimate=pl.CostEstimate(
            flops=18 * 10**9, bytes_accessed=8 * tokens * head_size * 2, transcendentals=6 * 10**6
        ),
        name="attend_back",
    )(order, received, grad, attended, log_total)


def place_weight(coords_ref, near, far, weight_v, sem):
    width = near[0].shape[2]
    for other, pieces in enumerate((near, far)):
        for dy, piece in enumerate(pieces):
            column = pl.multiple_of(lax.rem(coords_ref[0] + dy, SIDE) * width, 128)
            half = jnp.bitwise_xor(coords_ref[1], other)
            pltpu.make_async_copy(
                piece, weight_v.at[:, half, :, pl.ds(column, width)], sem
            ).start()


def project_back_kernel(coords_ref, cot_ref, *refs):
    near, far = refs[:SIDE], refs[SIDE : 2 * SIDE]
    out_ref, token_ref, weight_v, sem = refs[2 * SIDE :]
    place_weight(coords_ref, near, far, weight_v, sem)
    token_ref[...] = jnp.zeros_like(token_ref)
    pltpu.make_async_copy(weight_v, weight_v, sem).wait()
    heads = out_ref.shape[0] // 2
    rows, size = out_ref.shape[2:]
    for pair in range(heads // 2):
        grads = dot(
            cot_ref[...], weight_v[4 * pair : 4 * pair + 4].reshape(2 * size, -1), NT
        ).astype(BF16)
        for video in range(2):
            for one in range(2):
                out_ref[video * heads + pair * 2 + one, 0] = grads[
                    video * rows : (video + 1) * rows, one * size : (one + 1) * size
                ]


def weight_grad_kernel(coords_ref, att_ref, cot_ref, first_ref, keep_ref, send_ref):
    y, core = coords_ref[0], coords_ref[1]
    heads = att_ref.shape[0] // 2
    width = keep_ref.shape[2]
    cot = cot_ref[...]
    mine = jnp.broadcast_to(core == 0, (TILE, cot.shape[1]))
    for head in range(heads):
        both = jnp.concatenate([att_ref[head, 0], att_ref[heads + head, 0]], axis=0)
        part = lax.dot_general(both, cot, (((0,), (0,)), ((), ())), preferred_element_type=F32)
        keep = jnp.where(mine, part[:TILE], part[TILE:]).astype(BF16)
        send = jnp.where(mine, part[TILE:], part[:TILE]).astype(BF16)
        line = slice(head * TILE, (head + 1) * TILE)
        for block in range(SIDE):
            dy = lax.rem(block - y + SIDE, SIDE)
            columns = slice(block * width, (block + 1) * width)
            keep_ref[dy, line] = keep[:, columns]
            send_ref[dy, line] = send[:, columns]


def output_kernel(coords_ref, att_ref, *refs):
    near, far = refs[:SIDE], refs[SIDE : 2 * SIDE]
    first_ref, out_ref, weight_v, att_v, sem = refs[2 * SIDE :]
    place_weight(coords_ref, near, far, weight_v, sem)
    heads = att_ref.shape[0] // 2
    rows, size = att_ref.shape[2:]
    for head in range(heads):
        for video in range(2):
            att_v[video * rows : (video + 1) * rows, head * size : (head + 1) * size] = att_ref[
                video * heads + head, 0
            ]
    pltpu.make_async_copy(weight_v, weight_v, sem).wait()
    weight = weight_v[...].reshape(att_v.shape[1], -1)
    out_ref[...] = dot(att_v[...], weight).astype(BF16)


def project_back(coords, cot_rows, near, far, heads, size):
    rows, columns = cot_rows.shape
    units = 2 * heads
    return pl.pallas_call(
        project_back_kernel,
        out_shape=(jax.ShapeDtypeStruct((2 * heads, 1, rows // 2, size), BF16), TOKEN),
        in_specs=[SMEM, VMEM] + [ANYWHERE] * (2 * SIDE),
        out_specs=(VMEM, VMEM),
        scratch_shapes=[pltpu.VMEM((units, 2, TILE // 2, columns), BF16), pltpu.SemaphoreType.DMA],
        compiler_params=pltpu.CompilerParams(vmem_limit_bytes=VMEM_BYTES),
        cost_estimate=pl.CostEstimate(
            flops=2 * rows * columns * heads * size, bytes_accessed=9 * 10**6, transcendentals=0
        ),
        name="project_back",
    )(coords, cot_rows, *near, *far)


def weight_grad_parts(coords, attended, cot_rows, width, first):
    units, _, _, size = attended.shape
    rows, columns = cot_rows.shape
    half = jax.ShapeDtypeStruct((SIDE, units * size // 4, width), BF16)
    return pl.pallas_call(
        weight_grad_kernel,
        out_shape=(half, half),
        in_specs=[SMEM, VMEM, VMEM, VMEM],
        out_specs=(VMEM, VMEM),
        compiler_params=pltpu.CompilerParams(vmem_limit_bytes=40 * 1024 * 1024),
        cost_estimate=pl.CostEstimate(
            flops=rows * columns * units * size, bytes_accessed=8 * 10**6, transcendentals=0
        ),
        name="weight_grad_parts",
    )(coords, attended, cot_rows, first)


def project(coords, attended, columns, near, far, first):
    units, _, depth, size = attended.shape
    rows, heads = 2 * depth, units // 2
    return pl.pallas_call(
        output_kernel,
        out_shape=jax.ShapeDtypeStruct((rows, columns), BF16),
        in_specs=[SMEM, VMEM] + [ANYWHERE] * (2 * SIDE + 1),
        out_specs=VMEM,
        scratch_shapes=[
            pltpu.VMEM((units, 2, TILE // 2, columns), BF16), pltpu.VMEM((rows, heads * size), BF16),
            pltpu.SemaphoreType.DMA,
        ],
        compiler_params=pltpu.CompilerParams(vmem_limit_bytes=40 * 1024 * 1024),
        cost_estimate=pl.CostEstimate(
            flops=2 * rows * columns * heads * size, bytes_accessed=8 * 10**6, transcendentals=0
        ),
        name="project",
    )(coords, attended, *near, *far, first)


def along_y(array, step):
    return lax.ppermute(array, "dp", [(i, (i + step) % SIDE) for i in range(SIDE)])


def to_other_core(array):
    return lax.ppermute(array, "seq", [(i, i ^ 1) for i in range(lax.axis_size("seq"))])


def summed(terms):
    return functools.reduce(jnp.add, [t.astype(F32) for t in terms])


def scatter_near(keep, send):
    total = summed([keep, to_other_core(send)]).astype(BF16)
    half = total.shape[1] // 2
    passed = along_y(total[2, :half], 1), along_y(total[2, half:], -1)
    up = summed([total[1], jnp.pad(passed[0], ((0, half), (0, 0)))]).astype(BF16)
    down = summed([total[3], jnp.pad(passed[1], ((half, 0), (0, 0)))]).astype(BF16)
    return summed([total[0], along_y(up, 1), along_y(down, -1)]).astype(BF16)


def scatter_far(total):
    shards = lax.axis_size("seq")
    total = lax.all_to_all(
        total.reshape(shards // 2, TILE, -1), "seq", split_axis=0, concat_axis=0, tiled=True,
        axis_index_groups=[list(range(core, shards, 2)) for core in range(2)],
    )
    return jnp.sum(total.astype(F32), axis=0)


def gather_weight(block):
    shards = lax.axis_size("seq")
    depth, width = block.shape
    sent = jnp.broadcast_to(
        block.reshape(1, 2, depth // 2, width), (shards // 2, 2, depth // 2, width)
    )
    return exchange(sent.reshape(shards, depth // 2, width))


def pack_kernel(*refs):
    out_ref = refs[-1]
    for index, ref in enumerate(refs[:-1]):
        out_ref[:, index] = jnp.swapaxes(ref[...], 0, 1)


def pack(arrays):
    tokens, units, size = arrays[0].shape
    step = tokens // 4
    return pl.pallas_call(
        pack_kernel,
        grid=(4,),
        out_shape=jax.ShapeDtypeStruct((units, len(arrays), tokens, size), BF16),
        in_specs=[pl.BlockSpec((step, units, size), lambda i: (i, 0, 0))] * len(arrays),
        out_specs=pl.BlockSpec((units, len(arrays), step, size), lambda i: (0, 0, i, 0)),
        compiler_params=pltpu.CompilerParams(vmem_limit_bytes=VMEM_BYTES),
        name="pack",
    )(*arrays)


def unpack_kernel(in_ref, *refs):
    for index, ref in enumerate(refs):
        ref[...] = jnp.swapaxes(in_ref[:, index], 0, 1)


def unpack(array):
    units, count, tokens, size = array.shape
    step = tokens // 4
    return pl.pallas_call(
        unpack_kernel,
        grid=(4,),
        out_shape=[jax.ShapeDtypeStruct((tokens, units, size), BF16)] * count,
        in_specs=[pl.BlockSpec((units, count, step, size), lambda i: (0, 0, i, 0))],
        out_specs=[pl.BlockSpec((step, units, size), lambda i: (i, 0, 0))] * count,
        compiler_params=pltpu.CompilerParams(vmem_limit_bytes=40 * 1024 * 1024),
        name="unpack",
    )(array)


def after_kernel(array_ref, *refs):
    pass


def after(array, *first):
    return pl.pallas_call(
        after_kernel,
        out_shape=jax.ShapeDtypeStruct(array.shape, array.dtype),
        in_specs=[ANYWHERE] * (1 + len(first)),
        out_specs=ANYWHERE,
        input_output_aliases={0: 0},
        name="after",
    )(array, *first)


def exchange(array):
    return lax.all_to_all(array, "seq", split_axis=0, concat_axis=0, tiled=True)


def local(queries, keys_in, values_in, pair_keys, out_weight, cotangent):
    rows, videos, heads, head_size = queries.shape
    columns = cotangent.shape[2]
    coords = jnp.stack([lax.axis_index("dp"), lax.axis_index("seq") % 2]).astype(jnp.int32)
    units = videos * heads
    order = grid_order(pair_keys)
    cot_rows = jnp.transpose(cotangent, (1, 0, 2)).reshape(videos * rows, columns)
    packed = pack([a.reshape(rows, units, head_size) for a in (keys_in, values_in, queries)])
    block = gather_weight(out_weight)
    received = exchange(after(packed, block, order, cot_rows))
    half = block.shape[0] // 2
    up, down = along_y(block, -1), along_y(block, 1)
    opposite = jnp.concatenate([along_y(up[:half], -1), along_y(down[half:], 1)], axis=0)
    near = [block, up, opposite, down]
    far = [to_other_core(piece) for piece in near]
    grad_sent, token = project_back(coords, cot_rows, near, far, heads, head_size)
    grad_received = exchange(grad_sent)
    attended, attended_grid, log_total = attend(order, received, token)
    attended_tok = exchange(attended)
    grads_sent, token = attend_back(order, received, grad_received, attended_grid, log_total)
    total = scatter_near(
        *weight_grad_parts(coords, attended_tok, cot_rows, out_weight.shape[1], token)
    )
    output = project(coords, attended_tok, columns, near, far, total[:8])
    output = jnp.transpose(output.reshape(videos, rows, columns), (1, 0, 2))
    grad_k, grad_v, grad_q = (a.reshape(queries.shape) for a in unpack(exchange(grads_sent)))
    return output, grad_q, grad_k, grad_v, scatter_far(total)


def solution(mesh):
    placed = (
        P("seq", "dp", None, None),
        P("seq", "dp", None, None),
        P("seq", "dp", None, None),
        P(),
        P("seq", "dp"),
        P("seq", "dp", None),
    )
    return jax.shard_map(
        local,
        mesh=mesh,
        in_specs=placed,
        out_specs=(
            P("seq", "dp", None),
            P("seq", "dp", None, None),
            P("seq", "dp", None, None),
            P("seq", "dp", None, None),
            P("seq", "dp"),
        ),
        check_vma=False,
    )
```

```python
import functools

import jax
import jax.numpy as jnp
from jax import lax
from jax.experimental import pallas as pl
from jax.experimental.pallas import tpu as pltpu
from jax.sharding import PartitionSpec as P

F32, BF16 = jnp.float32, jnp.bfloat16
TILE = 64
SIDE = 4
ROW = SIDE * TILE
LOG2E = 1.4426950408889634
VMEM_BYTES = 60 * 1024 * 1024
NT = (((1,), (1,)), ((), ()))
NN = (((1,), (0,)), ((), ()))


def dot(a, b, dims=NN):
    return lax.dot_general(a, b, dims, preferred_element_type=F32)


def order_kernel(pairs_ref, order_ref):
    pairs = pairs_ref[...]
    tiles, slots = pairs.shape
    lane = lax.broadcasted_iota(jnp.int32, (tiles, tiles), 1)
    line = lax.broadcasted_iota(jnp.int32, (tiles, tiles), 0)
    near = jnp.zeros((tiles, tiles), F32)
    for slot in range(slots):
        near += (pairs[:, slot : slot + 1] == lane).astype(F32)
    near_b = near.astype(BF16)
    walks = dot(dot(near_b, near_b).astype(BF16), near_b)
    corner = jnp.sum(near, axis=0, keepdims=True) == 8.0
    ids = lane[:1]

    def first(mask):
        return jnp.min(jnp.where(mask, ids, tiles), axis=1, keepdims=True)

    def walks_from(tile):
        return jnp.sum(jnp.where(line == tile, walks, 0.0), axis=0, keepdims=True)

    base = walks_from(first(corner))
    ends = corner & (base == 16.0)
    place = jnp.zeros((1, tiles), jnp.int32)
    for _ in range(3):
        end = first(ends)
        ends = ends & (ids != end)
        far = walks_from(end)
        step = (
            (5.0 * far >= 3.0 * base).astype(jnp.int32)
            + (3.0 * far >= 5.0 * base).astype(jnp.int32)
            + (far >= 4.0 * base).astype(jnp.int32)
        )
        place = SIDE * place + step
    order_ref[...] = jnp.sum(jnp.where(place == line, lane, 0), axis=1, keepdims=True)


def grid_order(pair_keys):
    tiles = pair_keys.shape[0]
    return pl.pallas_call(
        order_kernel, out_shape=jax.ShapeDtypeStruct((tiles, 1), jnp.int32), name="grid_order"
    )(pair_keys).reshape(tiles)


def move_tiles(order_ref, remote, arrays, sem, inbound):
    @pl.loop(0, order_ref.shape[0])
    def _(place):
        tile = order_ref[place]
        far = remote.at[tile // 2, :, pl.ds(pl.multiple_of((tile % 2) * TILE, TILE), TILE)]
        here = arrays.at[:, pl.ds(pl.multiple_of(place * TILE, TILE), TILE)]
        if inbound:
            pltpu.make_async_copy(far, here, sem).start()
        else:
            pltpu.make_async_copy(here, far, sem).start()


def move_frame(order_ref, frame, remote, arrays, sem, inbound):
    for place in range(frame * SIDE * SIDE, (frame + 1) * SIDE * SIDE):
        tile = order_ref[place]
        far = remote.at[tile // 2, :, pl.ds(pl.multiple_of((tile % 2) * TILE, TILE), TILE)]
        here = arrays.at[:, place * TILE : (place + 1) * TILE]
        if inbound:
            pltpu.make_async_copy(far, here, sem).start()
        else:
            pltpu.make_async_copy(here, far, sem).start()


def await_tiles(arrays, sem):
    pltpu.make_async_copy(arrays, arrays, sem).wait()


def transposed(source, target):
    for block in range(source.shape[0] // ROW):
        rows = pl.ds(block * ROW, ROW)
        target[:, rows] = source[rows, :].T


def window(r):
    low, high = max(r - 1, 0), min(r + 1, SIDE - 1)
    return low, high - low + 1


STARTS = [sum(window(i)[1] for i in range(r)) for r in range(SIDE + 1)]
LEFT = (slice(0, 3 * TILE), slice(0, 2 * TILE))
RIGHT = (slice(TILE, 4 * TILE), slice(2 * TILE, 4 * TILE))


def masked(scores, b):
    block = scores[b * ROW : (b + 1) * ROW]
    left, right = block[LEFT], block[RIGHT]
    first = lax.broadcasted_iota(jnp.int32, (TILE, 2 * TILE), 1) < TILE
    left = jnp.concatenate([left[: 2 * TILE], jnp.where(first, -jnp.inf, left[2 * TILE :])], axis=0)
    right = jnp.concatenate([jnp.where(first, right[:TILE], -jnp.inf), right[TILE:]], axis=0)
    return left, right


def sides(row):
    return row[:, : 2 * TILE], row[:, 2 * TILE :]


def rows_of(frame, r, count=1):
    return pl.ds((frame * SIDE + r) * ROW, count * ROW)


def span(frame):
    return slice(frame * SIDE * ROW, (frame + 1) * SIDE * ROW)


def frames_near(frame):
    return range(max(frame - 1, 0), min(frame + 2, SIDE))


def forward_kernel(
    scale, order_ref, recv_ref, token_ref, out_ref, grid_ref, log_ref,
    kvq_v, vt_v, weights_v, top_v, total_v, acc_v, in_sem, out_sem,
):
    move_tiles(order_ref, recv_ref, kvq_v, in_sem, True)
    weights_v[...] = jnp.zeros_like(weights_v)
    await_tiles(kvq_v, in_sem)
    transposed(kvq_v.at[1], vt_v)
    factor = scale * LOG2E

    for frame in range(SIDE):
        top_v[...] = jnp.full_like(top_v, -jnp.inf)
        total_v[...] = jnp.zeros_like(total_v)
        acc_v[...] = jnp.zeros_like(acc_v)

        for other in frames_near(frame):
            def score(r):
                low, count = window(r)
                return dot(kvq_v[0, rows_of(other, low, count)], kvq_v[2, rows_of(frame, r)], NT)

            def weigh(r, scores):
                low, count = window(r)
                parts = [masked(scores, b) for b in range(count)]
                top = top_v[r : r + 1]
                highest = [
                    functools.reduce(
                        jnp.maximum, [jnp.max(p[side], axis=0, keepdims=True) for p in parts]
                    )
                    for side in range(2)
                ]
                new_top = jnp.maximum(top, jnp.concatenate(highest, axis=1) * factor)
                fade = jnp.exp2(top - new_top)
                tops = sides(new_top)
                sums = [0.0, 0.0]
                for b, p in enumerate(parts):
                    for side, where in enumerate((LEFT, RIGHT)):
                        e = jnp.exp2(p[side] * factor - tops[side])
                        sums[side] += jnp.sum(e, axis=0, keepdims=True)
                        weights_v[(STARTS[r] + b,) + where] = e.astype(BF16)
                total_v[r : r + 1] = total_v[r : r + 1] * fade + jnp.concatenate(sums, axis=1)
                top_v[r : r + 1] = new_top
                weights = weights_v[STARTS[r] : STARTS[r + 1]].reshape(count * ROW, ROW)
                acc_v[r] = acc_v[r] * fade + dot(vt_v[:, rows_of(other, low, count)], weights)

            ahead = score(0)
            for r in range(SIDE):
                scores, ahead = ahead, score(r + 1) if r + 1 < SIDE else None
                weigh(r, scores)

        for r in range(SIDE):
            total = total_v[r : r + 1]
            grid_ref[0, rows_of(frame, r)] = (acc_v[r] / total).T.astype(BF16)
            log_ref[frame, r : r + 1] = top_v[r : r + 1] + jnp.log2(total)

    move_tiles(order_ref, out_ref, grid_ref, out_sem, False)
    await_tiles(grid_ref, out_sem)


def backward_kernel(
    scale, order_ref, recv_ref, grad_ref, att_ref, log_ref, out_ref, token_ref,
    kvq_v, g_v, out_v, kt_v, dk_acc, dv_acc, weights_v, slopes_v, acc_v, in_sem, grad_sem, out_sem,
):
    head_size = kvq_v.shape[2]
    for frame in range(SIDE):
        move_frame(order_ref, frame, recv_ref, kvq_v, in_sem.at[frame], True)
        move_frame(order_ref, frame, grad_ref, g_v, grad_sem.at[frame], True)
    weights_v[...] = jnp.zeros_like(weights_v)
    slopes_v[...] = jnp.zeros_like(slopes_v)
    dk_acc[...] = jnp.zeros_like(dk_acc)
    dv_acc[...] = jnp.zeros_like(dv_acc)
    factor = scale * LOG2E
    ones = jnp.ones((8, head_size), BF16)

    def arrive(frame):
        rows = span(frame)
        await_tiles(kvq_v.at[:, rows], in_sem.at[frame])
        await_tiles(g_v.at[:, rows], grad_sem.at[frame])
        for r in range(SIDE):
            kt_v[:, rows_of(frame, r)] = kvq_v[0, rows_of(frame, r)].T

    def leave(frame):
        rows = span(frame)
        out_v[0, rows] = (dk_acc[rows] * scale).astype(BF16)
        out_v[1, rows] = dv_acc[rows].astype(BF16)
        move_frame(order_ref, frame, out_ref, out_v, out_sem, False)

    arrive(0)

    for frame in range(SIDE):
        acc_v[...] = jnp.zeros_like(acc_v)
        deltas, logs = [], []
        for r in range(SIDE):
            rows = rows_of(frame, r)
            product = g_v[0, rows].astype(F32) * att_ref[0, rows].astype(F32)
            upper = product.astype(BF16)
            lower = (product - upper.astype(F32)).astype(BF16)
            deltas.append(sides((dot(ones, upper, NT) + dot(ones, lower, NT))[:1]))
            logs.append(sides(log_ref[frame, r : r + 1]))

        for other in frames_near(frame):
            if other > frame:
                arrive(other)

            def score(r):
                low, count = window(r)
                keys = rows_of(other, low, count)
                rows = rows_of(frame, r)
                return (
                    dot(kvq_v[0, keys], kvq_v[2, rows], NT),
                    dot(kvq_v[1, keys], g_v[0, rows], NT),
                )

            def weigh(r, scores, grad_probs):
                low, count = window(r)
                for b in range(count):
                    parts = masked(scores, b)
                    block = grad_probs[b * ROW : (b + 1) * ROW]
                    for side, where in enumerate((LEFT, RIGHT)):
                        probs = jnp.exp2(parts[side] * factor - logs[r][side])
                        slopes = probs * (block[where] - deltas[r][side])
                        weights_v[(STARTS[r] + b,) + where] = probs.astype(BF16)
                        slopes_v[(STARTS[r] + b,) + where] = slopes.astype(BF16)
                slopes = slopes_v[STARTS[r] : STARTS[r + 1]].reshape(count * ROW, ROW)
                acc_v[r] += dot(kt_v[:, rows_of(other, low, count)], slopes)

            def collect(key_r):
                low, count = window(key_r)
                picks = [STARTS[r] + key_r - window(r)[0] for r in range(low, low + count)]
                keys = rows_of(other, key_r)
                rows = rows_of(frame, low, count)
                dv_acc[keys] += dot(
                    jnp.concatenate([weights_v[b] for b in picks], axis=1), g_v[0, rows]
                )
                dk_acc[keys] += dot(
                    jnp.concatenate([slopes_v[b] for b in picks], axis=1), kvq_v[2, rows]
                )

            ahead = score(0)
            for r in range(SIDE):
                now, ahead = ahead, score(r + 1) if r + 1 < SIDE else None
                weigh(r, *now)
                if r > 0:
                    collect(r - 1)
            collect(SIDE - 1)

        for r in range(SIDE):
            out_v[2, rows_of(frame, r)] = (acc_v[r] * scale).T.astype(BF16)

        if frame > 0:
            leave(frame - 1)
    leave(SIDE - 1)
    token_ref[...] = jnp.zeros_like(token_ref)
    await_tiles(out_v, out_sem)


SMEM = pl.BlockSpec(memory_space=pltpu.SMEM)
ANYWHERE = pl.BlockSpec(memory_space=pl.ANY)
VMEM = pl.BlockSpec(memory_space=pltpu.VMEM)
TOKEN = jax.ShapeDtypeStruct((8, 128), F32)


def attend(order, received, token):
    shards, _, rows, head_size = received.shape
    tokens = shards * rows
    square = pltpu.VMEM((STARTS[SIDE], ROW, ROW), BF16)
    return pl.pallas_call(
        functools.partial(forward_kernel, head_size**-0.5),
        out_shape=(
            jax.ShapeDtypeStruct((shards, 1, rows, head_size), BF16),
            jax.ShapeDtypeStruct((1, tokens, head_size), BF16),
            jax.ShapeDtypeStruct((SIDE, SIDE, ROW), F32),
        ),
        in_specs=[SMEM, ANYWHERE, VMEM],
        out_specs=(ANYWHERE, VMEM, VMEM),
        scratch_shapes=[
            pltpu.VMEM((3, tokens, head_size), BF16), pltpu.VMEM((head_size, tokens), BF16), square,
            pltpu.VMEM((SIDE, ROW), F32), pltpu.VMEM((SIDE, ROW), F32),
            pltpu.VMEM((SIDE, head_size, ROW), F32),
            pltpu.SemaphoreType.DMA, pltpu.SemaphoreType.DMA,
        ],
        compiler_params=pltpu.CompilerParams(vmem_limit_bytes=VMEM_BYTES),
        cost_estimate=pl.CostEstimate(
            flops=8 * 10**9, bytes_accessed=4 * tokens * head_size * 2, transcendentals=6 * 10**6
        ),
        name="attend",
    )(order, received, token)


def attend_back(order, received, grad, attended, log_total):
    shards, _, rows, head_size = received.shape
    tokens = shards * rows
    square = pltpu.VMEM((STARTS[SIDE], ROW, ROW), BF16)
    total = pltpu.VMEM((tokens, head_size), F32)
    return pl.pallas_call(
        functools.partial(backward_kernel, head_size**-0.5),
        out_shape=(jax.ShapeDtypeStruct((shards, 3, rows, head_size), BF16), TOKEN),
        in_specs=[SMEM, ANYWHERE, ANYWHERE, VMEM, VMEM],
        out_specs=(ANYWHERE, VMEM),
        scratch_shapes=[
            pltpu.VMEM((3, tokens, head_size), BF16), pltpu.VMEM((1, tokens, head_size), BF16),
            pltpu.VMEM((3, tokens, head_size), BF16),
            pltpu.VMEM((head_size, tokens), BF16), total, total, square, square,
            pltpu.VMEM((SIDE, head_size, ROW), F32),
            pltpu.SemaphoreType.DMA((SIDE,)), pltpu.SemaphoreType.DMA((SIDE,)), pltpu.SemaphoreType.DMA,
        ],
        compiler_params=pltpu.CompilerParams(vmem_limit_bytes=VMEM_BYTES),
        cost_estimate=pl.CostEstimate(
            flops=18 * 10**9, bytes_accessed=8 * tokens * head_size * 2, transcendentals=6 * 10**6
        ),
        name="attend_back",
    )(order, received, grad, attended, log_total)


def place_weight(coords_ref, near, far, weight_v, sem):
    width = near[0].shape[2]
    for other, pieces in enumerate((near, far)):
        for dy, piece in enumerate(pieces):
            column = pl.multiple_of(lax.rem(coords_ref[0] + dy, SIDE) * width, 128)
            half = jnp.bitwise_xor(coords_ref[1], other)
            pltpu.make_async_copy(
                piece, weight_v.at[:, half, :, pl.ds(column, width)], sem
            ).start()


def project_back_kernel(coords_ref, cot_ref, *refs):
    near, far = refs[:SIDE], refs[SIDE : 2 * SIDE]
    out_ref, token_ref, weight_v, sem = refs[2 * SIDE :]
    place_weight(coords_ref, near, far, weight_v, sem)
    token_ref[...] = jnp.zeros_like(token_ref)
    pltpu.make_async_copy(weight_v, weight_v, sem).wait()
    heads = out_ref.shape[0] // 2
    rows, size = out_ref.shape[2:]
    for pair in range(heads // 2):
        grads = dot(
            cot_ref[...], weight_v[4 * pair : 4 * pair + 4].reshape(2 * size, -1), NT
        ).astype(BF16)
        for video in range(2):
            for one in range(2):
                out_ref[video * heads + pair * 2 + one, 0] = grads[
                    video * rows : (video + 1) * rows, one * size : (one + 1) * size
                ]


def weight_grad_kernel(coords_ref, att_ref, cot_ref, first_ref, keep_ref, out_ref, send_ref, sems):
    y, core = coords_ref[0], coords_ref[1]
    heads = att_ref.shape[0] // 2
    width = keep_ref.shape[2]
    cot = cot_ref[...]
    mine = jnp.broadcast_to(core == 0, (TILE, cot.shape[1]))
    copies = []
    for head in range(heads):
        both = jnp.concatenate([att_ref[head, 0], att_ref[heads + head, 0]], axis=0)
        part = lax.dot_general(both, cot, (((0,), (0,)), ((), ())), preferred_element_type=F32)
        keep = jnp.where(mine, part[:TILE], part[TILE:]).astype(BF16)
        send = jnp.where(mine, part[TILE:], part[:TILE]).astype(BF16)
        line = slice(head * TILE, (head + 1) * TILE)
        for block in range(SIDE):
            dy = lax.rem(block - y + SIDE, SIDE)
            columns = slice(block * width, (block + 1) * width)
            keep_ref[dy, line] = keep[:, columns]
            send_ref[dy, line] = send[:, columns]
        if head % SIDE == SIDE - 1:
            done = slice((head + 1 - SIDE) * TILE, (head + 1) * TILE)
            copies.append(
                pltpu.make_async_copy(
                    send_ref.at[:, done], out_ref.at[:, done], sems.at[head // SIDE]
                )
            )
            copies[-1].start()
    for copy in copies:
        copy.wait()


def output_kernel(coords_ref, att_ref, *refs):
    near, far = refs[:SIDE], refs[SIDE : 2 * SIDE]
    first_ref, out_ref, weight_v, att_v, sem = refs[2 * SIDE :]
    place_weight(coords_ref, near, far, weight_v, sem)
    heads = att_ref.shape[0] // 2
    rows, size = att_ref.shape[2:]
    for head in range(heads):
        for video in range(2):
            att_v[video * rows : (video + 1) * rows, head * size : (head + 1) * size] = att_ref[
                video * heads + head, 0
            ]
    pltpu.make_async_copy(weight_v, weight_v, sem).wait()
    weight = weight_v[...].reshape(att_v.shape[1], -1)
    out_ref[...] = dot(att_v[...], weight).astype(BF16)


def project_back(coords, cot_rows, near, far, heads, size):
    rows, columns = cot_rows.shape
    units = 2 * heads
    return pl.pallas_call(
        project_back_kernel,
        out_shape=(jax.ShapeDtypeStruct((2 * heads, 1, rows // 2, size), BF16), TOKEN),
        in_specs=[SMEM, VMEM] + [ANYWHERE] * (2 * SIDE),
        out_specs=(VMEM, VMEM),
        scratch_shapes=[pltpu.VMEM((units, 2, TILE // 2, columns), BF16), pltpu.SemaphoreType.DMA],
        compiler_params=pltpu.CompilerParams(vmem_limit_bytes=VMEM_BYTES),
        cost_estimate=pl.CostEstimate(
            flops=2 * rows * columns * heads * size, bytes_accessed=9 * 10**6, transcendentals=0
        ),
        name="project_back",
    )(coords, cot_rows, *near, *far)


def weight_grad_parts(coords, attended, cot_rows, width, first):
    units, _, _, size = attended.shape
    rows, columns = cot_rows.shape
    heads = units // 2
    half = jax.ShapeDtypeStruct((SIDE, units * size // 4, width), BF16)
    return pl.pallas_call(
        weight_grad_kernel,
        out_shape=(half, half),
        in_specs=[SMEM, VMEM, VMEM, VMEM],
        out_specs=(VMEM, ANYWHERE),
        scratch_shapes=[
            pltpu.VMEM(half.shape, BF16), pltpu.SemaphoreType.DMA((heads // SIDE,))
        ],
        compiler_params=pltpu.CompilerParams(vmem_limit_bytes=40 * 1024 * 1024),
        cost_estimate=pl.CostEstimate(
            flops=rows * columns * units * size, bytes_accessed=8 * 10**6, transcendentals=0
        ),
        name="weight_grad_parts",
    )(coords, attended, cot_rows, first)


def project(coords, attended, columns, near, far, first):
    units, _, depth, size = attended.shape
    rows, heads = 2 * depth, units // 2
    return pl.pallas_call(
        output_kernel,
        out_shape=jax.ShapeDtypeStruct((rows, columns), BF16),
        in_specs=[SMEM, VMEM] + [ANYWHERE] * (2 * SIDE + 1),
        out_specs=VMEM,
        scratch_shapes=[
            pltpu.VMEM((units, 2, TILE // 2, columns), BF16), pltpu.VMEM((rows, heads * size), BF16),
            pltpu.SemaphoreType.DMA,
        ],
        compiler_params=pltpu.CompilerParams(vmem_limit_bytes=40 * 1024 * 1024),
        cost_estimate=pl.CostEstimate(
            flops=2 * rows * columns * heads * size, bytes_accessed=8 * 10**6, transcendentals=0
        ),
        name="project",
    )(coords, attended, *near, *far, first)


def along_y(array, step):
    return lax.ppermute(array, "dp", [(i, (i + step) % SIDE) for i in range(SIDE)])


def to_other_core(array):
    return lax.ppermute(array, "seq", [(i, i ^ 1) for i in range(lax.axis_size("seq"))])


def summed(terms):
    return functools.reduce(jnp.add, [t.astype(F32) for t in terms])


def scatter_near(keep, send):
    total = summed([keep, to_other_core(send)]).astype(BF16)
    half = total.shape[1] // 2
    passed = along_y(total[2, :half], 1), along_y(total[2, half:], -1)
    up = summed([total[1], jnp.pad(passed[0], ((0, half), (0, 0)))]).astype(BF16)
    down = summed([total[3], jnp.pad(passed[1], ((half, 0), (0, 0)))]).astype(BF16)
    return summed([total[0], along_y(up, 1), along_y(down, -1)]).astype(BF16)


def scatter_far(total):
    shards = lax.axis_size("seq")
    total = lax.all_to_all(
        total.reshape(shards // 2, TILE, -1), "seq", split_axis=0, concat_axis=0, tiled=True,
        axis_index_groups=[list(range(core, shards, 2)) for core in range(2)],
    )
    return jnp.sum(total.astype(F32), axis=0)


def gather_weight(block):
    shards = lax.axis_size("seq")
    depth, width = block.shape
    sent = jnp.broadcast_to(
        block.reshape(1, 2, depth // 2, width), (shards // 2, 2, depth // 2, width)
    )
    return exchange(sent.reshape(shards, depth // 2, width))


def pack_kernel(*refs):
    out_ref = refs[-1]
    for index, ref in enumerate(refs[:-1]):
        out_ref[:, index] = jnp.swapaxes(ref[...], 0, 1)


def pack(arrays):
    tokens, units, size = arrays[0].shape
    step = tokens // 4
    return pl.pallas_call(
        pack_kernel,
        grid=(4,),
        out_shape=jax.ShapeDtypeStruct((units, len(arrays), tokens, size), BF16),
        in_specs=[pl.BlockSpec((step, units, size), lambda i: (i, 0, 0))] * len(arrays),
        out_specs=pl.BlockSpec((units, len(arrays), step, size), lambda i: (0, 0, i, 0)),
        compiler_params=pltpu.CompilerParams(vmem_limit_bytes=VMEM_BYTES),
        name="pack",
    )(*arrays)


def unpack_kernel(in_ref, *refs):
    for index, ref in enumerate(refs):
        ref[...] = jnp.swapaxes(in_ref[:, index], 0, 1)


def unpack(array):
    units, count, tokens, size = array.shape
    step = tokens // 4
    return pl.pallas_call(
        unpack_kernel,
        grid=(4,),
        out_shape=[jax.ShapeDtypeStruct((tokens, units, size), BF16)] * count,
        in_specs=[pl.BlockSpec((units, count, step, size), lambda i: (0, 0, i, 0))],
        out_specs=[pl.BlockSpec((step, units, size), lambda i: (i, 0, 0))] * count,
        compiler_params=pltpu.CompilerParams(vmem_limit_bytes=40 * 1024 * 1024),
        name="unpack",
    )(array)


def after_kernel(array_ref, *refs):
    pass


def after(array, *first):
    return pl.pallas_call(
        after_kernel,
        out_shape=jax.ShapeDtypeStruct(array.shape, array.dtype),
        in_specs=[ANYWHERE] * (1 + len(first)),
        out_specs=ANYWHERE,
        input_output_aliases={0: 0},
        name="after",
    )(array, *first)


def exchange(array):
    return lax.all_to_all(array, "seq", split_axis=0, concat_axis=0, tiled=True)


def local(queries, keys_in, values_in, pair_keys, out_weight, cotangent):
    rows, videos, heads, head_size = queries.shape
    columns = cotangent.shape[2]
    coords = jnp.stack([lax.axis_index("dp"), lax.axis_index("seq") % 2]).astype(jnp.int32)
    units = videos * heads
    order = grid_order(pair_keys)
    cot_rows = jnp.transpose(cotangent, (1, 0, 2)).reshape(videos * rows, columns)
    packed = pack([a.reshape(rows, units, head_size) for a in (keys_in, values_in, queries)])
    block = gather_weight(out_weight)
    received = exchange(after(packed, block, order, cot_rows))
    half = block.shape[0] // 2
    up, down = along_y(block, -1), along_y(block, 1)
    opposite = jnp.concatenate([along_y(up[:half], -1), along_y(down[half:], 1)], axis=0)
    near = [block, up, opposite, down]
    far = [to_other_core(piece) for piece in near]
    grad_sent, token = project_back(coords, cot_rows, near, far, heads, head_size)
    grad_received = exchange(grad_sent)
    attended, attended_grid, log_total = attend(order, received, token)
    attended_tok = exchange(attended)
    grads_sent, token = attend_back(order, received, grad_received, attended_grid, log_total)
    total = scatter_near(
        *weight_grad_parts(coords, attended_tok, cot_rows, out_weight.shape[1], token)
    )
    output = project(coords, attended_tok, columns, near, far, total[:8])
    output = jnp.transpose(output.reshape(videos, rows, columns), (1, 0, 2))
    grad_k, grad_v, grad_q = (a.reshape(queries.shape) for a in unpack(exchange(grads_sent)))
    return output, grad_q, grad_k, grad_v, scatter_far(total)


def solution(mesh):
    placed = (
        P("seq", "dp", None, None),
        P("seq", "dp", None, None),
        P("seq", "dp", None, None),
        P(),
        P("seq", "dp"),
        P("seq", "dp", None),
    )
    return jax.shard_map(
        local,
        mesh=mesh,
        in_specs=placed,
        out_specs=(
            P("seq", "dp", None),
            P("seq", "dp", None, None),
            P("seq", "dp", None, None),
            P("seq", "dp", None, None),
            P("seq", "dp"),
        ),
        check_vma=False,
    )
```
